32 devices in a mesh: mem: 4 (over y, x), space: 8 (over z, core).
Axes of the slice: x: 2, y: 2, z: 4, core: 2. Of those that a mesh axis runs over, the one named last changes fastest.
Arguments:
- log_perm: float32 [8, 32, 128, 128], P('mem', 'space'), may hold values from -4 to 4
- saturation: float32 [32, 128, 128], P('space'), may hold values from 0.1 to 0.9
- pressure_init: float32 [32, 128, 128], P('space'), may hold values from -3 to 3
- wells: int32 [64], replicated, may hold values from 0 to 524287
- well_rate: float32 [64], replicated, may hold values from -4 to 4
- obs_index: int32 [512, 8], replicated, may hold values from 0 to 524287, as said below
- obs_weight: float32 [512, 8], replicated, may hold values from -2 to 2
- obs_value: float32 [512], replicated, may hold values from -5 to 5
- obs_var: float32 [512], replicated, may hold values from 0.1 to 1
- noise: float32 [8, 512], replicated, may hold values from -5 to 5
Outputs:
- updated_perm: float32 [8, 32, 128, 128], P(None, 'space', 'mem')
The draws below stay inside these ranges and needn't reach their ends.
Inputs may be any that keep to these rules, and one draw needn't show every extreme that they name: `obs_index`: observation o reads only cells of the grid row o % 32 along the first dimension.
All inputs are finite; a program needn't handle non-finite values.
Results may differ from the reference program's by a relative error of at most 0.00007.
Values sent between devices are 32-bit elements; how exact they have to be, the bound alone decides.
A program may use at most 128 MiB of HBM per device.

```python
import math
import jax
import jax.numpy as jnp
from jax import lax

NY = 128
NZ = 128
SWEEPS = 6
NOBS = 512
TAPS = 8
WELLS = 64
ENS = 8
NX = 32


def well_cells(key):
    first = jax.random.randint(jax.random.fold_in(key, 11), (WELLS,), 0, NX)
    second = jax.random.randint(jax.random.fold_in(key, 12), (WELLS,), 0, NY)
    third = jax.random.randint(jax.random.fold_in(key, 13), (WELLS,), 0, NZ)
    return (first, second, third)


def draw_wells(key, part):
    first, second, third = well_cells(key)
    return ((first * NY + second) * NZ + third).astype(jnp.int32)


def draw_obs_index(key, part):
    row = (jnp.arange(NOBS) % NX).astype(jnp.int32)
    centre_y = jax.random.randint(jax.random.fold_in(key, 21), (NOBS,), 0, NY)
    centre_z = jax.random.randint(jax.random.fold_in(key, 22), (NOBS,), 0, NZ)
    offsets = jax.random.randint(jax.random.fold_in(key, 23), (NOBS, TAPS, 2), -2, 3)
    cell_y = jnp.clip(centre_y[:, None] + offsets[:, :, 0], 0, NY - 1)
    cell_z = jnp.clip(centre_z[:, None] + offsets[:, :, 1], 0, NZ - 1)
    return ((row[:, None] * NY + cell_y) * NZ + cell_z).astype(jnp.int32)


def block_levels(key, dims, pieces, least, high):
    level, own = 1.0, jax.random.fold_in(key, 6)
    for position, parts in pieces:
        draws = jnp.exp(jax.random.uniform(jax.random.fold_in(own, position), (parts,), jnp.float32, least / len(pieces), high / len(pieces)))
        level = level * jnp.repeat(draws, dims[position] // parts).reshape([-1 if axis == position else 1 for axis in range(len(dims))])
    return level


def gaussian(stream_key, extent, width, most, pieces=(), dtype=jnp.bfloat16):
    result = width * jax.random.normal(stream_key, extent, jnp.float32)
    if pieces:
        result = result * block_levels(stream_key, extent, pieces, -0.22, 0.18)
    return jnp.clip(result, -most, most).astype(dtype)


def setup_inputs(seed: int = 0) -> dict:
    key_of = jax.random.split(jax.random.key(seed), 11)
    log_perm = gaussian(key_of[0], (ENS, NX, NY, NZ), 1.0, 4.0, ((0, 4), (1, 8)), jnp.float32)
    saturation = jnp.clip(0.1 + 0.79999997 * jax.random.uniform(key_of[1], (NX, NY, NZ), jnp.float32) ** block_levels(key_of[1], (NX, NY, NZ), ((0, 8),), -0.2, 0.2), 0.1, 0.9)
    pressure_init = gaussian(key_of[2], (NX, NY, NZ), 0.5, 3.0, ((0, 8),), jnp.float32)
    wells = draw_wells(jax.random.fold_in(key_of[10], 71), 0)
    well_rate = jnp.clip(jax.random.uniform(key_of[4], (WELLS,), jnp.float32, -4.0, 4.0), -4.0, 4.0)
    obs_index = draw_obs_index(jax.random.fold_in(key_of[10], 71), 0)
    obs_weight = gaussian(key_of[6], (NOBS, TAPS), TAPS ** -0.5, 2.0, (), jnp.float32)
    obs_value = gaussian(key_of[7], (NOBS,), 1.0, 5.0, (), jnp.float32)
    obs_var = jnp.clip(jnp.exp(jax.random.uniform(key_of[8], (NOBS,), jnp.float32, math.log(0.1), math.log(1.0))), 0.1, 1.0)
    noise = gaussian(key_of[9], (ENS, NOBS), 1.0, 5.0, (), jnp.float32)
    return dict(log_perm=log_perm, saturation=saturation, pressure_init=pressure_init, wells=wells, well_rate=well_rate, obs_index=obs_index, obs_weight=obs_weight, obs_value=obs_value, obs_var=obs_var, noise=noise)


water_visc = 1.0
oil_visc = 4.0
time_step = 0.1
storage = 1.0
inflation = 4.0

def pad_cells(field):
    return jnp.pad(field, ((1, 1), (1, 1), (1, 1)))

def beside_all(field):
    return [field[2:, 1:-1, 1:-1], field[:-2, 1:-1, 1:-1], field[1:-1, 2:, 1:-1], field[1:-1, :-2, 1:-1], field[1:-1, 1:-1, 2:], field[1:-1, 1:-1, :-2]]

def middle(field):
    return field[1:-1, 1:-1, 1:-1]

def props(perm, sat):
    water = sat * sat / water_visc
    oil = (1.0 - sat) * (1.0 - sat) / oil_visc
    total = water + oil
    return (perm * total, water / total)

def saturate(perm_pad, sat_pad, press_pad, source):
    lam, frac = props(perm_pad, sat_pad)
    lam_mid, frac_mid, press_mid = (middle(lam), middle(frac), middle(press_pad))
    outflow = jnp.zeros_like(lam_mid)
    for lam_next, frac_next, press_next in zip(beside_all(lam), beside_all(frac), beside_all(press_pad)):
        flux = 0.5 * (lam_mid + lam_next) * (press_mid - press_next)
        outflow = outflow + jnp.maximum(flux, 0.0) * frac_mid + jnp.minimum(flux, 0.0) * frac_next
    water = jnp.maximum(source, 0.0) + jnp.minimum(source, 0.0) * frac_mid
    return jnp.clip(middle(sat_pad) + time_step * (water - outflow), 0.0, 1.0)

def pressure(perm_pad, sat_pad, press_pad, source):
    lam, frac = props(perm_pad, sat_pad)
    lam_mid = middle(lam)
    numer = storage * middle(press_pad) + source
    denom = storage + jnp.zeros_like(lam_mid)
    for lam_next, press_next in zip(beside_all(lam), beside_all(press_pad)):
        trans = 0.5 * (lam_mid + lam_next)
        numer = numer + trans * press_next
        denom = denom + trans
    return numer / denom

def reference(log_perm, saturation, pressure_init, wells, well_rate, obs_index, obs_weight, obs_value, obs_var, noise):
    source = jnp.zeros((NX * NY * NZ,), jnp.float32).at[wells].add(well_rate).reshape(NX, NY, NZ)

    def member(member_log):
        perm_pad = pad_cells(jnp.exp(member_log))
        sat, press = (saturation, pressure_init)
        for sweep in range(SWEEPS):
            sat = saturate(perm_pad, pad_cells(sat), pad_cells(press), source)
            press = pressure(perm_pad, pad_cells(sat), pad_cells(press), source)
        flat = press.reshape(-1)
        return lax.optimization_barrier(jnp.sum(obs_weight * flat[obs_index], axis=1))
    predicted = lax.map(member, log_perm)
    high = lax.Precision.HIGHEST
    dev = predicted - lax.optimization_barrier(jnp.mean(predicted, axis=0, keepdims=True))
    cov = jnp.dot(dev.T, dev, precision=high) / (ENS - 1) + inflation * jnp.diag(obs_var)
    resid = obs_value[None, :] + jnp.sqrt(inflation * obs_var)[None, :] * noise - predicted
    factor = jnp.linalg.cholesky(cov)
    half = lax.linalg.triangular_solve(factor, resid.T, left_side=True, lower=True)
    solved = lax.linalg.triangular_solve(factor, half, left_side=True, lower=True, transpose_a=True)
    weights = jnp.dot(dev, solved, precision=high) / (ENS - 1)
    spread = log_perm - lax.optimization_barrier(jnp.mean(log_perm, axis=0, keepdims=True))
    return log_perm + jnp.tensordot(weights.T, spread, axes=1, precision=high)
```

```python
import functools

import jax
import jax.numpy as jnp
from jax import lax
from jax.experimental import pallas as pl
from jax.experimental.pallas import tpu as pltpu
from jax.sharding import PartitionSpec as P

SWEEPS = 6
time_step = 0.1
inflation = 4.0

MESH = pl.DeviceIdType.MESH
HIGH = lax.Precision.HIGHEST
SUB = 8
LANES = 128
CHUNK = 4


def iota(shape, dim):
    return lax.broadcasted_iota(jnp.int32, shape, dim)


def as_float(cond):
    return jnp.where(cond, 1.0, 0.0).astype(jnp.float32)


def kernel(
    n_mem,
    n_space,
    lp,
    sat,
    pre,
    wells,
    rate,
    oi,
    ow,
    ov,
    var,
    noise,
    out,
    S,
    L,
    F,
    Q,
    half_perm,
    src,
    lp_ghost,
    sat_ghost,
    pre_ghost,
    cols,
    pred,
    gram,
    first_send,
    first_recv,
    s_send,
    s_recv,
    p_send,
    p_recv,
    col_send,
    col_recv,
    pred_send,
    pred_recv,
    gram_send,
    gram_recv,
):
    members, width, ny, nz = lp.shape
    yl = ny // SUB
    part = ny // n_mem
    ens = members * n_mem
    total_rows = width * n_space
    nobs = oi.shape[1]
    taps = oi.shape[0]
    per_row = nobs // total_rows
    row_taps = taps * per_row
    local_obs = per_row * width
    plane = ny * nz
    mem = lax.axis_index("mem")
    place = lax.axis_index("space")
    has_left = place > 0
    has_right = place < n_space - 1

    barrier = pltpu.get_barrier_semaphore()
    for d in range(1, n_mem):
        pl.semaphore_signal(
            barrier, inc=1, device_id=(lax.rem(mem + d, n_mem), place), device_id_type=MESH
        )
    for d in range(1, n_space):
        pl.semaphore_signal(
            barrier, inc=1, device_id=(mem, lax.rem(place + d, n_space)), device_id_type=MESH
        )

    def clear(row, side):
        S[:, :, row] = jnp.zeros_like(S[:, :, row])
        Q[:, :, row] = jnp.zeros_like(Q[:, :, row])
        lp_ghost[side] = jnp.zeros_like(lp_ghost[side])
        sat_ghost[side] = jnp.zeros_like(sat_ghost[side])
        pre_ghost[side] = jnp.zeros_like(pre_ghost[side])

    @pl.when(jnp.logical_not(has_left))
    def _():
        clear(0, 0)

    @pl.when(jnp.logical_not(has_right))
    def _():
        clear(width + 1, 1)

    pl.semaphore_wait(barrier, n_mem - 1 + n_space - 1)

    def remote(a, b, send, recv, target):
        return pltpu.make_async_remote_copy(
            src_ref=a, dst_ref=b, send_sem=send, recv_sem=recv, device_id=target, device_id_type=MESH
        )

    right = (mem, lax.rem(place + 1, n_space))
    left = (mem, lax.rem(place + n_space - 1, n_space))

    def first(side):
        row = width - 1 if side == 0 else 0
        target = right if side == 0 else left
        pairs = [
            (pre.at[row], pre_ghost.at[side]),
            (sat.at[row], sat_ghost.at[side]),
            (lp.at[:, row], lp_ghost.at[side]),
        ]
        return [
            remote(a, b, first_send.at[side, i], first_recv.at[side, i], target)
            for i, (a, b) in enumerate(pairs)
        ]

    def halo(field, send, recv, k, m, side):
        a = width if side == 0 else 1
        b = 0 if side == 0 else width + 1
        rows = pl.ds(1, yl)
        return remote(
            field.at[k, m, a, rows],
            field.at[k, m, b, rows],
            send.at[k, m, side],
            recv.at[k, m, side],
            right if side == 0 else left,
        )

    def each(make, to_do, sending):
        for side in (0, 1):
            there = (has_right, has_left)[side if sending else 1 - side]

            @pl.when(there)
            def _(side=side):
                for copy in make(side):
                    getattr(copy, to_do)()

    each(first, "start", True)

    def column(d):
        peer = lax.rem(mem + d, n_mem)
        return remote(
            lp.at[:, :, pl.ds(pl.multiple_of(peer * part, part), part)],
            cols.at[pl.ds(mem * members, members)],
            col_send.at[d],
            col_recv.at[d],
            (peer, place),
        )

    for d in range(1, n_mem):
        column(d).start()
    for m in range(members):
        cols[mem * members + m] = lp[m, :, pl.ds(pl.multiple_of(mem * part, part), part)]

    def strided(ref, lead, c):
        return ref[(*lead, pl.ds(c, SUB, stride=yl), slice(None))]

    def props(half, s):
        water = s * s
        dry = 1.0 - s
        total = water + dry * dry * 0.25
        return half * total, water / total

    sub = iota((SUB, nz), 0)
    lane = iota((SUB, nz), 1)
    inner = as_float(lane < nz - 1)
    not_first = as_float(lane > 0)
    ends = as_float((lane == 0) | (lane == nz - 1))
    sub_first = sub == 0
    sub_last = sub == SUB - 1

    def pads(field, k, m, r):
        top = field[k, m, r, yl]
        field[k, m, r, 0] = jnp.where(sub_first, 0.0, pltpu.roll(top, 1, 0))
        bottom = field[k, m, r, 1]
        field[k, m, r, yl + 1] = jnp.where(sub_last, 0.0, pltpu.roll(bottom, SUB - 1, 0))

    def load_row(m, r):
        for c in range(yl):
            half = 0.5 * jnp.exp(strided(lp, (m, r), c))
            s = strided(sat, (r,), c)
            lam, frac = props(half, s)
            half_perm[m, r + 1, c] = half
            S[0, m, r + 1, c + 1] = s
            L[0, m, r + 1, c + 1] = lam
            F[0, m, r + 1, c + 1] = frac
            Q[0, m, r + 1, c + 1] = strided(pre, (r,), c)
        pads(L, 0, m, r + 1)
        pads(F, 0, m, r + 1)
        pads(Q, 0, m, r + 1)

    for m in range(members):

        @pl.loop(0, width)
        def _(r, m=m):
            load_row(m, r)

    well = wells[...].astype(jnp.float32)
    well_x = jnp.floor((well + 0.5) * (1.0 / plane))
    rest = well - well_x * plane
    well_y = jnp.floor((rest + 0.5) * (1.0 / nz))
    well_z = rest - well_y * nz
    count = well.shape[1]
    pos = iota((ny, count), 0)
    held_y = ((pos % SUB) * yl + pos // SUB).astype(jnp.float32)
    at_z = as_float(pos.astype(jnp.float32) == well_z)
    at_y = held_y == well_y
    for r in range(width):
        here = well_x == (place * width + r).astype(jnp.float32)
        at_row = jnp.where(at_y & here, rate[...], 0.0)
        field = lax.dot_general(
            at_row, at_z, (((1,), (1,)), ((), ())), precision=HIGH, preferred_element_type=jnp.float32
        )
        src[r] = field.reshape(yl, SUB, nz)

    def dot(a, b):
        return jnp.dot(a, b, precision=HIGH, preferred_element_type=jnp.float32)

    index_all = oi[...].astype(jnp.float32)
    weight_all = ow[...]
    from_obs = iota((nobs, row_taps), 0)
    tap_lane = iota((nobs, row_taps), 1)
    own_tap = iota((taps, row_taps), 0) == iota((taps, row_taps), 1) // per_row
    tap_pos = iota((ny, row_taps), 0)
    tap_y = ((tap_pos % SUB) * yl + tap_pos // SUB).astype(jnp.float32)
    tap_z = tap_pos.astype(jnp.float32)
    z_hot, y_hot, gather_taps = [], [], []
    for r in range(width):
        x = place * width + r
        select = as_float(from_obs == x + total_rows * (tap_lane % per_row))
        index = jnp.sum(jnp.where(own_tap, dot(index_all, select), 0.0), axis=0, keepdims=True)
        weight = jnp.sum(jnp.where(own_tap, dot(weight_all, select), 0.0), axis=0, keepdims=True)
        rest = index - (x * plane).astype(jnp.float32)
        cell_y = jnp.floor((rest + 0.5) * (1.0 / nz))
        cell_z = rest - cell_y * nz
        z_hot.append(as_float(tap_z == cell_z))
        y_hot.append(jnp.where(tap_y == cell_y, weight, 0.0))
        gather_taps.append(
            as_float(
                iota((row_taps, LANES), 1) == r * per_row + iota((row_taps, LANES), 0) % per_row
            )
        )
    obs_lane = iota((nobs, LANES), 1)
    own_obs = as_float(
        (iota((nobs, LANES), 0) == place * width + obs_lane // per_row + total_rows * (obs_lane % per_row))
        & (obs_lane < local_obs)
    )
    noise_own = dot(noise[...], own_obs)
    value_own = dot(jnp.broadcast_to(ov[...], (SUB, nobs)), own_obs)
    var_own = dot(jnp.broadcast_to(var[...], (SUB, nobs)), own_obs)

    each(first, "wait_recv", False)
    for side in (0, 1):
        row = 0 if side == 0 else width + 1
        there = as_float(has_left if side == 0 else has_right)
        for c in range(yl):
            s = strided(sat_ghost, (side,), c)
            p = strided(pre_ghost, (side,), c)
            for m in range(members):
                half = 0.5 * there * jnp.exp(strided(lp_ghost, (side, m), c))
                lam, frac = props(half, s)
                half_perm[m, row, c] = half
                L[0, m, row, c + 1] = lam
                F[0, m, row, c + 1] = frac
                Q[0, m, row, c + 1] = p

    def beside(field, k, m, r, c):
        mid = pl.ds(1 + c, CHUNK)
        return [
            field[k, m, r + 1, mid],
            field[k, m, r - 1, mid],
            field[k, m, r, pl.ds(c + 2, CHUNK)],
            field[k, m, r, pl.ds(c, CHUNK)],
        ]

    def saturate(k, m, r):
        for c in range(0, yl, CHUNK):
            mid = pl.ds(1 + c, CHUNK)
            lam, frac, press = L[k, m, r, mid], F[k, m, r, mid], Q[k, m, r, mid]
            lam_next = pltpu.roll(lam, nz - 1, 2)
            frac_next = pltpu.roll(frac, nz - 1, 2)
            press_next = pltpu.roll(press, nz - 1, 2)
            flux = (lam + lam_next) * inner * (press - press_next)
            along = flux * jnp.where(flux > 0.0, frac, frac_next)
            outflow = along - pltpu.roll(along, 1, 2)
            outflow = outflow + ends * jnp.maximum(lam * press, 0.0) * frac
            for lam_j, frac_j, press_j in zip(
                beside(L, k, m, r, c), beside(F, k, m, r, c), beside(Q, k, m, r, c)
            ):
                flux = (lam + lam_j) * (press - press_j)
                outflow = outflow + flux * jnp.where(flux > 0.0, frac, frac_j)
            source = src[r - 1, pl.ds(c, CHUNK)]
            water = jnp.maximum(source, 0.0) + jnp.minimum(source, 0.0) * frac
            s = jnp.clip(S[k, m, r, mid] + time_step * (water - outflow), 0.0, 1.0)
            lam, frac = props(half_perm[m, r, pl.ds(c, CHUNK)], s)
            S[k + 1, m, r, mid] = s
            L[k + 1, m, r, mid] = lam
            F[k + 1, m, r, mid] = frac
        pads(L, k + 1, m, r)
        pads(F, k + 1, m, r)

    def pressure(k, m, r):
        for c in range(0, yl, CHUNK):
            mid = pl.ds(1 + c, CHUNK)
            lam, press = L[k + 1, m, r, mid], Q[k, m, r, mid]
            lam_j = beside(L, k + 1, m, r, c) + [
                pltpu.roll(lam, 1, 2) * not_first,
                pltpu.roll(lam, nz - 1, 2) * inner,
            ]
            press_j = beside(Q, k, m, r, c) + [
                pltpu.roll(press, 1, 2) * not_first,
                pltpu.roll(press, nz - 1, 2) * inner,
            ]
            denom = 1.0 + 6.0 * lam + sum(lam_j[1:], lam_j[0])
            numer = press + src[r - 1, pl.ds(c, CHUNK)] + lam * sum(press_j[1:], press_j[0])
            for a, b in zip(lam_j, press_j):
                numer = numer + a * b
            Q[k + 1, m, r, mid] = numer / denom
        pads(Q, k + 1, m, r)

    def ghost_props(k, m, row):
        for c in range(0, yl, CHUNK):
            mid = pl.ds(1 + c, CHUNK)
            lam, frac = props(half_perm[m, row, pl.ds(c, CHUNK)], S[k, m, row, mid])
            L[k, m, row, mid] = lam
            F[k, m, row, mid] = frac

    def s_halo(k, m):
        return lambda side: [halo(S, s_send, s_recv, k, m, side)]

    def p_halo(k, m):
        return lambda side: [halo(Q, p_send, p_recv, k, m, side)]

    def inside(step, k, m):
        @pl.loop(2, width)
        def _(r):
            step(k, m, r)

    def border(step, k, m):
        @pl.loop(0, 2)
        def _(i):
            step(k, m, 1 + i * (width - 1))

    @pl.loop(0, SWEEPS)
    def _(k):
        for m in range(members):
            inside(saturate, k, m)
        for m in range(members):

            @pl.when(k > 0)
            def _(m=m):
                each(p_halo(k, m), "wait_recv", False)

            border(saturate, k, m)
            each(s_halo(k + 1, m), "start", True)
        for m in range(members):
            inside(pressure, k, m)
        for m in range(members):
            each(s_halo(k + 1, m), "wait_recv", False)

            @pl.loop(0, 2)
            def _(i, m=m):
                ghost_props(k + 1, m, i * (width + 1))

            border(pressure, k, m)

            @pl.when(k + 1 < SWEEPS)
            def _(m=m):
                each(p_halo(k + 1, m), "start", True)

    member_row = iota((ens, LANES), 0)
    own = jnp.zeros((ens, LANES), jnp.float32)
    for r in range(width):
        found = jnp.zeros((ens, row_taps), jnp.float32)
        for m in range(members):
            field = Q[SWEEPS, m, r + 1, pl.ds(1, yl)].reshape(ny, nz)
            picked = jnp.sum(dot(field, z_hot[r]) * y_hot[r], axis=0, keepdims=True)
            found = jnp.where(iota((ens, row_taps), 0) == mem * members + m, picked, found)
        own = own + dot(found, gather_taps[r])
    pred[mem] = own

    def share(d):
        return remote(
            pred.at[mem], pred.at[mem], pred_send.at[d], pred_recv.at[d], (lax.rem(mem + d, n_mem), place)
        )

    for d in range(1, n_mem):
        share(d).start()
    scale = jnp.where(iota((ens, LANES), 1) < local_obs, inflation * var_own, 1.0)
    inverse = jnp.where(iota((ens, LANES), 1) < local_obs, 1.0 / scale, 0.0)
    target_obs = value_own + jnp.sqrt(inflation * var_own) * noise_own
    for d in range(1, n_mem):
        share(d).wait_recv()
    predicted = pred[0]
    for a in range(1, n_mem):
        predicted = predicted + pred[a]
    dev = predicted - jnp.mean(predicted, axis=0, keepdims=True)
    resid = target_obs - predicted
    both = jnp.concatenate([dev, resid, jnp.zeros((LANES - 2 * ens, LANES), jnp.float32)], axis=0)
    gram[place] = lax.dot_general(
        dev * inverse, both, (((1,), (1,)), ((), ())), precision=HIGH, preferred_element_type=jnp.float32
    )

    def sum_part(d):
        return remote(
            gram.at[place],
            gram.at[place],
            gram_send.at[d],
            gram_recv.at[d],
            (mem, lax.rem(place + d, n_space)),
        )

    for d in range(1, n_space):
        sum_part(d).start()
    for d in range(1, n_mem):
        column(d).wait_recv()
    for d in range(1, n_space):
        sum_part(d).wait_recv()
    whole = gram[0]
    for a in range(1, n_space):
        whole = whole + gram[a]

    row_id = iota((ens, LANES), 0)
    lane_id = iota((ens, LANES), 1)
    table = whole / (ens - 1) + as_float(row_id == lane_id)
    for i in range(ens):
        pivot_row = table[i : i + 1, :] / table[i : i + 1, i : i + 1]
        table = jnp.where(row_id == i, pivot_row, table - table[:, i : i + 1] * pivot_row)
    mixing = (
        table - jnp.mean(table, axis=0, keepdims=True) + as_float(row_id + ens == lane_id)
    )
    for m in range(ens):
        factors = [
            jnp.broadcast_to(mixing[j : j + 1, ens + m : ens + m + 1], (SUB, nz)) for j in range(ens)
        ]
        for r in range(width):
            for c in range(0, part, SUB):
                total = factors[0] * cols[0, r, pl.ds(c, SUB)]
                for j in range(1, ens):
                    total = total + factors[j] * cols[j, r, pl.ds(c, SUB)]
                out[m, r, pl.ds(c, SUB)] = total

    each(first, "wait_send", True)
    for d in range(1, n_mem):
        column(d).wait_send()
        share(d).wait_send()
    for d in range(1, n_space):
        sum_part(d).wait_send()

    @pl.loop(1, SWEEPS + 1)
    def _(k):
        for m in range(members):
            each(s_halo(k, m), "wait_send", True)

            @pl.when(k < SWEEPS)
            def _(m=m):
                each(p_halo(k, m), "wait_send", True)


def body(
    log_perm,
    saturation,
    pressure_init,
    wells,
    well_rate,
    obs_index,
    obs_weight,
    obs_value,
    obs_var,
    noise,
):
    n_mem = lax.axis_size("mem")
    n_space = lax.axis_size("space")
    members, width, ny, nz = log_perm.shape
    ens = members * n_mem
    yl = ny // SUB
    part = ny // n_mem
    vmem = pl.BlockSpec(memory_space=pltpu.VMEM)
    state = pltpu.VMEM((SWEEPS + 1, members, width + 2, yl + 2, SUB, nz), jnp.float32)
    dma = pltpu.SemaphoreType.DMA
    return pl.pallas_call(
        functools.partial(kernel, n_mem, n_space),
        out_shape=jax.ShapeDtypeStruct((ens, width, part, nz), jnp.float32),
        in_specs=[vmem] * 10,
        out_specs=vmem,
        scratch_shapes=[
            state,
            state,
            state,
            state,
            pltpu.VMEM((members, width + 2, yl, SUB, nz), jnp.float32),
            pltpu.VMEM((width, yl, SUB, nz), jnp.float32),
            pltpu.VMEM((2, members, ny, nz), jnp.float32),
            pltpu.VMEM((2, ny, nz), jnp.float32),
            pltpu.VMEM((2, ny, nz), jnp.float32),
            pltpu.VMEM((ens, width, part, nz), jnp.float32),
            pltpu.VMEM((n_mem, ens, LANES), jnp.float32),
            pltpu.VMEM((n_space, ens, LANES), jnp.float32),
            dma((2, 3)),
            dma((2, 3)),
            dma((SWEEPS + 1, members, 2)),
            dma((SWEEPS + 1, members, 2)),
            dma((SWEEPS + 1, members, 2)),
            dma((SWEEPS + 1, members, 2)),
            dma((n_mem,)),
            dma((n_mem,)),
            dma((n_mem,)),
            dma((n_mem,)),
            dma((n_space,)),
            dma((n_space,)),
        ],
        compiler_params=pltpu.CompilerParams(
            collective_id=0, has_side_effects=True, vmem_limit_bytes=48 * 1024 * 1024
        ),
    )(
        log_perm,
        saturation,
        pressure_init,
        wells[None],
        well_rate[None],
        obs_index.T,
        obs_weight.T,
        obs_value[None],
        obs_var[None],
        noise,
    )


def solution(mesh):
    placed = (
        P("mem", "space", None, None),
        P("space", None, None),
        P("space", None, None),
        P(),
        P(),
        P(),
        P(),
        P(),
        P(),
        P(),
    )
    return jax.shard_map(
        body, mesh=mesh, in_specs=placed, out_specs=P(None, "space", "mem", None), check_vma=False
    )
```

```python
import functools

import jax
import jax.numpy as jnp
from jax import lax
from jax.experimental import pallas as pl
from jax.experimental.pallas import tpu as pltpu
from jax.sharding import PartitionSpec as P

SWEEPS = 6
time_step = 0.1
inflation = 4.0

MESH = pl.DeviceIdType.MESH
HIGH = lax.Precision.HIGHEST
SUB = 8
LANES = 128
CHUNK = 4
PARTS = 2


def iota(shape, dim):
    return lax.broadcasted_iota(jnp.int32, shape, dim)


def as_float(cond):
    return jnp.where(cond, 1.0, 0.0).astype(jnp.float32)


def split_dot(a, hot):
    rows = a.shape[0]
    high = a.astype(jnp.bfloat16).astype(jnp.float32)
    rest = a - high
    middle = rest.astype(jnp.bfloat16).astype(jnp.float32)
    terms = jnp.concatenate([high, middle, rest - middle], axis=0).astype(jnp.bfloat16)
    got = jnp.dot(terms, hot.astype(jnp.bfloat16), preferred_element_type=jnp.float32)
    return got[:rows] + got[rows : 2 * rows] + got[2 * rows :]


def kernel(
    n_mem,
    n_space,
    lp_in,
    sat_in,
    pre_in,
    wells_in,
    rate_in,
    oi_in,
    ow_in,
    ov_in,
    var_in,
    noise_in,
    out,
    lp,
    sat,
    pre,
    wells,
    rate,
    oi,
    ow,
    ov,
    var,
    noise,
    z_hot,
    y_hot,
    tap_sum,
    obs_own,
    local_sem,
    S,
    L,
    F,
    Q,
    half_perm,
    src,
    lp_ghost,
    sat_ghost,
    pre_ghost,
    cols,
    pred,
    gram,
    first_send,
    first_recv,
    s_send,
    s_recv,
    p_send,
    p_recv,
    col_send,
    col_recv,
    pred_send,
    pred_recv,
    gram_send,
    gram_recv,
):
    members, width, ny, nz = lp.shape
    yl = ny // SUB
    part = ny // n_mem
    ens = members * n_mem
    total_rows = width * n_space
    nobs = oi.shape[1]
    taps = oi.shape[0]
    per_row = nobs // total_rows
    row_taps = taps * per_row
    local_obs = per_row * width
    plane = ny * nz
    mem = lax.axis_index("mem")
    place = lax.axis_index("space")
    has_left = place > 0
    has_right = place < n_space - 1

    arrivals = [
        pltpu.make_async_copy(a, b, local_sem.at[i])
        for i, (a, b) in enumerate(
            [
                (pre_in, pre),
                (sat_in, sat),
                (lp_in, lp),
                (wells_in, wells),
                (rate_in, rate),
                (oi_in, oi),
                (ow_in, ow),
                (ov_in, ov),
                (var_in, var),
                (noise_in, noise),
                (
                    lp_in.at[:, :, pl.ds(pl.multiple_of(mem * part, part), part)],
                    cols.at[pl.ds(mem * members, members)],
                ),
            ]
        )
    ]
    for copy in arrivals:
        copy.start()

    barrier = pltpu.get_barrier_semaphore()
    for d in range(1, n_mem):
        pl.semaphore_signal(
            barrier, inc=1, device_id=(lax.rem(mem + d, n_mem), place), device_id_type=MESH
        )
    for d in range(1, n_space):
        pl.semaphore_signal(
            barrier, inc=1, device_id=(mem, lax.rem(place + d, n_space)), device_id_type=MESH
        )

    def clear(row, side):
        S[:, :, row] = jnp.zeros_like(S[:, :, row])
        Q[:, :, row] = jnp.zeros_like(Q[:, :, row])
        lp_ghost[side] = jnp.zeros_like(lp_ghost[side])
        sat_ghost[side] = jnp.zeros_like(sat_ghost[side])
        pre_ghost[side] = jnp.zeros_like(pre_ghost[side])

    @pl.when(jnp.logical_not(has_left))
    def _():
        clear(0, 0)

    @pl.when(jnp.logical_not(has_right))
    def _():
        clear(width + 1, 1)

    pl.semaphore_wait(barrier, n_mem - 1 + n_space - 1)

    def remote(a, b, send, recv, target):
        return pltpu.make_async_remote_copy(
            src_ref=a, dst_ref=b, send_sem=send, recv_sem=recv, device_id=target, device_id_type=MESH
        )

    right = (mem, lax.rem(place + 1, n_space))
    left = (mem, lax.rem(place + n_space - 1, n_space))

    def first(side):
        row = width - 1 if side == 0 else 0
        target = right if side == 0 else left
        pairs = [
            (pre_in.at[row], pre_ghost.at[side]),
            (sat_in.at[row], sat_ghost.at[side]),
            (lp_in.at[:, row], lp_ghost.at[side]),
        ]
        return [
            remote(a, b, first_send.at[side, i], first_recv.at[side, i], target)
            for i, (a, b) in enumerate(pairs)
        ]

    piece = yl // PARTS

    def halo(field, send, recv, k, m, h, side):
        a = width if side == 0 else 1
        b = 0 if side == 0 else width + 1
        rows = pl.ds(1 + h * piece, piece)
        return remote(
            field.at[k, m, a, rows],
            field.at[k, m, b, rows],
            send.at[k, m, h, side],
            recv.at[k, m, h, side],
            right if side == 0 else left,
        )

    def each(make, to_do, sending):
        for side in (0, 1):
            there = (has_right, has_left)[side if sending else 1 - side]

            @pl.when(there)
            def _(side=side):
                for copy in make(side):
                    getattr(copy, to_do)()

    each(first, "start", True)

    def column(d):
        peer = lax.rem(mem + d, n_mem)
        return remote(
            lp_in.at[:, :, pl.ds(pl.multiple_of(peer * part, part), part)],
            cols.at[pl.ds(mem * members, members)],
            col_send.at[d],
            col_recv.at[d],
            (peer, place),
        )

    for d in range(1, n_mem):
        column(d).start()
    for copy in arrivals:
        copy.wait()

    def strided(ref, lead, c):
        return ref[(*lead, pl.ds(c, SUB, stride=yl), slice(None))]

    def props(half, s):
        water = s * s
        dry = 1.0 - s
        total = water + dry * dry * 0.25
        return half * total, water / total

    sub = iota((SUB, nz), 0)
    lane = iota((SUB, nz), 1)
    inner = as_float(lane < nz - 1)
    not_first = as_float(lane > 0)
    ends = as_float((lane == 0) | (lane == nz - 1))
    sub_first = sub == 0
    sub_last = sub == SUB - 1

    def pads(field, k, m, r):
        top = field[k, m, r, yl]
        field[k, m, r, 0] = jnp.where(sub_first, 0.0, pltpu.roll(top, 1, 0))
        bottom = field[k, m, r, 1]
        field[k, m, r, yl + 1] = jnp.where(sub_last, 0.0, pltpu.roll(bottom, SUB - 1, 0))

    def load_row(m, r):
        for c in range(yl):
            half = 0.5 * jnp.exp(strided(lp, (m, r), c))
            s = strided(sat, (r,), c)
            lam, frac = props(half, s)
            half_perm[m, r + 1, c] = half
            S[0, m, r + 1, c + 1] = s
            L[0, m, r + 1, c + 1] = lam
            F[0, m, r + 1, c + 1] = frac
            Q[0, m, r + 1, c + 1] = strided(pre, (r,), c)
        pads(L, 0, m, r + 1)
        pads(F, 0, m, r + 1)
        pads(Q, 0, m, r + 1)

    for m in range(members):

        @pl.loop(0, width)
        def _(r, m=m):
            load_row(m, r)

    well = wells[...].astype(jnp.float32)
    well_x = jnp.floor((well + 0.5) * (1.0 / plane))
    rest = well - well_x * plane
    well_y = jnp.floor((rest + 0.5) * (1.0 / nz))
    well_z = rest - well_y * nz
    count = well.shape[1]

    def held_y(lanes):
        shape = (yl, SUB, lanes)
        return (iota(shape, 1) * yl + iota(shape, 0)).astype(jnp.float32).reshape(ny, lanes)

    at_z = as_float(iota((nz, count), 0).astype(jnp.float32) == well_z)
    at_y = held_y(count) == well_y
    for r in range(width):
        here = well_x == (place * width + r).astype(jnp.float32)
        at_row = jnp.where(at_y & here, rate[...], 0.0)
        field = lax.dot_general(
            at_row, at_z, (((1,), (1,)), ((), ())), precision=HIGH, preferred_element_type=jnp.float32
        )
        src[r] = field.reshape(yl, SUB, nz)

    def tables(r):
        x = place * width + r
        tap_lane = iota((1, row_taps), 1)
        select = as_float(iota((nobs, row_taps), 0) == x + total_rows * (tap_lane % per_row))
        both = jnp.concatenate([oi[...].astype(jnp.float32), ow[...]], axis=0)
        found = split_dot(both, select)
        own_tap = iota((taps, row_taps), 0) == tap_lane // per_row
        index = jnp.sum(jnp.where(own_tap, found[:taps], 0.0), axis=0, keepdims=True)
        weight = jnp.sum(jnp.where(own_tap, found[taps:], 0.0), axis=0, keepdims=True)
        rest = index - (x * plane).astype(jnp.float32)
        cell_y = jnp.floor((rest + 0.5) * (1.0 / nz))
        cell_z = rest - cell_y * nz
        z_hot[r] = as_float(iota((nz, row_taps), 0).astype(jnp.float32) == cell_z)
        y_hot[r] = jnp.where(held_y(row_taps) == cell_y, weight, 0.0)
        tap_sum[r] = as_float(
            iota((row_taps, LANES), 1) == r * per_row + iota((row_taps, 1), 0) % per_row
        )

    def own_data():
        lane = iota((1, LANES), 1)
        cell = place * width + lane // per_row + total_rows * (lane % per_row)
        select = as_float(iota((nobs, LANES), 0) == jnp.where(lane < local_obs, cell, -1))
        rows = [jnp.broadcast_to(ov[...], (SUB, nobs)), jnp.broadcast_to(var[...], (SUB, nobs))]
        pad = jnp.zeros((16 - ens % 16, nobs), jnp.float32)
        obs_own[...] = split_dot(jnp.concatenate(rows + [noise[...], pad], axis=0), select)

    def first_ghosts():
        each(first, "wait_recv", False)
        for side in (0, 1):
            row = 0 if side == 0 else width + 1
            there = as_float(has_left if side == 0 else has_right)
            for c in range(yl):
                s = strided(sat_ghost, (side,), c)
                p = strided(pre_ghost, (side,), c)
                for m in range(members):
                    half = 0.5 * there * jnp.exp(strided(lp_ghost, (side, m), c))
                    lam, frac = props(half, s)
                    half_perm[m, row, c] = half
                    L[0, m, row, c + 1] = lam
                    F[0, m, row, c + 1] = frac
                    Q[0, m, row, c + 1] = p

    def slab(field, k, m, r, c):
        return field[k, m, r, pl.ds(c, CHUNK + 2)]

    def saturate(k, m, r, lo, hi):
        for c in range(lo, hi, CHUNK):
            mid = pl.ds(1 + c, CHUNK)
            lam_y, frac_y, press_y = slab(L, k, m, r, c), slab(F, k, m, r, c), slab(Q, k, m, r, c)
            lam, frac, press = lam_y[1:-1], frac_y[1:-1], press_y[1:-1]
            flux = (lam_y[:-1] + lam_y[1:]) * (press_y[:-1] - press_y[1:])
            along = flux * jnp.where(flux > 0.0, frac_y[:-1], frac_y[1:])
            outflow = along[1:] - along[:-1]
            for row in (r - 1, r + 1):
                flux = (lam + L[k, m, row, mid]) * (press - Q[k, m, row, mid])
                outflow = outflow + flux * jnp.where(flux > 0.0, frac, F[k, m, row, mid])
            lam_next = pltpu.roll(lam, nz - 1, 2)
            frac_next = pltpu.roll(frac, nz - 1, 2)
            press_next = pltpu.roll(press, nz - 1, 2)
            flux = (lam + lam_next) * inner * (press - press_next)
            along = flux * jnp.where(flux > 0.0, frac, frac_next)
            outflow = outflow + (along - pltpu.roll(along, 1, 2))
            outflow = outflow + ends * jnp.maximum(lam * press, 0.0) * frac
            source = src[r - 1, pl.ds(c, CHUNK)]
            water = jnp.maximum(source, 0.0) + jnp.minimum(source, 0.0) * frac
            s = jnp.clip(S[k, m, r, mid] + time_step * (water - outflow), 0.0, 1.0)
            lam, frac = props(half_perm[m, r, pl.ds(c, CHUNK)], s)
            S[k + 1, m, r, mid] = s
            L[k + 1, m, r, mid] = lam
            F[k + 1, m, r, mid] = frac

    def saturate_pads(k, m, r):
        pads(L, k + 1, m, r)
        pads(F, k + 1, m, r)

    def pressure(k, m, r, lo, hi):
        for c in range(lo, hi, CHUNK):
            mid = pl.ds(1 + c, CHUNK)
            lam_y, press_y = slab(L, k + 1, m, r, c), slab(Q, k, m, r, c)
            both_y = lam_y * press_y
            lam, press = lam_y[1:-1], press_y[1:-1]
            numer = press + src[r - 1, pl.ds(c, CHUNK)] + both_y[2:] + both_y[:-2]
            lam_sum = lam_y[2:] + lam_y[:-2]
            press_sum = press_y[2:] + press_y[:-2]
            others = [(L[k + 1, m, row, mid], Q[k, m, row, mid]) for row in (r - 1, r + 1)]
            others.append((pltpu.roll(lam, 1, 2) * not_first, pltpu.roll(press, 1, 2) * not_first))
            others.append((pltpu.roll(lam, nz - 1, 2) * inner, pltpu.roll(press, nz - 1, 2) * inner))
            for a, b in others:
                numer = numer + a * b
                lam_sum = lam_sum + a
                press_sum = press_sum + b
            Q[k + 1, m, r, mid] = (numer + lam * press_sum) / (1.0 + 6.0 * lam + lam_sum)

    def pressure_pads(k, m, r):
        pads(Q, k + 1, m, r)

    def ghost_props(k, m, row, lo, hi):
        for c in range(lo, hi, CHUNK):
            mid = pl.ds(1 + c, CHUNK)
            lam, frac = props(half_perm[m, row, pl.ds(c, CHUNK)], S[k, m, row, mid])
            L[k, m, row, mid] = lam
            F[k, m, row, mid] = frac

    def s_halo(k, m, h):
        return lambda side: [halo(S, s_send, s_recv, k, m, h, side)]

    def p_halo(k, m, h):
        return lambda side: [halo(Q, p_send, p_recv, k, m, h, side)]

    def inside(step, finish, k, m):
        @pl.loop(2, width)
        def _(r):
            step(k, m, r, 0, yl)
            finish(k, m, r)

    def border(step, finish, k, m, h):
        @pl.loop(0, 2)
        def _(i):
            r = 1 + i * (width - 1)
            step(k, m, r, h * piece, (h + 1) * piece)
            if h == PARTS - 1:
                finish(k, m, r)

    halves = [(m, h) for m in range(members) for h in range(PARTS)]

    @pl.loop(0, SWEEPS)
    def _(k):
        for m in range(members):
            inside(saturate, saturate_pads, k, m)

        @pl.when(k == 0)
        def _():
            first_ghosts()

        for m, h in halves:

            @pl.when(k > 0)
            def _(m=m, h=h):
                each(p_halo(k, m, h), "wait_recv", False)

            border(saturate, saturate_pads, k, m, h)
            each(s_halo(k + 1, m, h), "start", True)
        for m in range(members):
            inside(pressure, pressure_pads, k, m)

        @pl.when(k < width)
        def _():
            tables(k)

        @pl.when(k == SWEEPS - 1)
        def _():
            own_data()

        for m, h in halves:
            each(s_halo(k + 1, m, h), "wait_recv", False)

            @pl.loop(0, 2)
            def _(i, m=m, h=h):
                ghost_props(k + 1, m, i * (width + 1), h * piece, (h + 1) * piece)

            border(pressure, pressure_pads, k, m, h)

            @pl.when(k + 1 < SWEEPS)
            def _(m=m, h=h):
                each(p_halo(k + 1, m, h), "start", True)

    own = jnp.zeros((ens, LANES), jnp.float32)
    for r in range(width):
        found = jnp.zeros((ens, row_taps), jnp.float32)
        fields = Q[SWEEPS, :, r + 1, pl.ds(1, yl)].reshape(members * ny, nz)
        columns = split_dot(fields, z_hot[r])
        for m in range(members):
            picked = jnp.sum(columns[m * ny : (m + 1) * ny] * y_hot[r], axis=0, keepdims=True)
            found = jnp.where(iota((ens, row_taps), 0) == mem * members + m, picked, found)
        own = own + split_dot(found, tap_sum[r])
    pred[mem] = own

    def share(d):
        return remote(
            pred.at[mem], pred.at[mem], pred_send.at[d], pred_recv.at[d], (lax.rem(mem + d, n_mem), place)
        )

    for d in range(1, n_mem):
        share(d).start()
    value_own, var_own = obs_own[:SUB], obs_own[SUB : 2 * SUB]
    noise_own = obs_own[2 * SUB : 2 * SUB + ens]
    scale = jnp.where(iota((ens, LANES), 1) < local_obs, inflation * var_own, 1.0)
    inverse = jnp.where(iota((ens, LANES), 1) < local_obs, 1.0 / scale, 0.0)
    target_obs = value_own + jnp.sqrt(inflation * var_own) * noise_own
    for d in range(1, n_mem):
        share(d).wait_recv()
    predicted = pred[0]
    for a in range(1, n_mem):
        predicted = predicted + pred[a]
    dev = predicted - jnp.mean(predicted, axis=0, keepdims=True)
    resid = target_obs - predicted
    both = jnp.concatenate([dev, resid, jnp.zeros((LANES - 2 * ens, LANES), jnp.float32)], axis=0)
    gram[place] = lax.dot_general(
        dev * inverse, both, (((1,), (1,)), ((), ())), precision=HIGH, preferred_element_type=jnp.float32
    )

    def sum_part(d):
        return remote(
            gram.at[place],
            gram.at[place],
            gram_send.at[d],
            gram_recv.at[d],
            (mem, lax.rem(place + d, n_space)),
        )

    for d in range(1, n_space):
        sum_part(d).start()
    for d in range(1, n_mem):
        column(d).wait_recv()
    for d in range(1, n_space):
        sum_part(d).wait_recv()
    whole = gram[0]
    for a in range(1, n_space):
        whole = whole + gram[a]

    row_id = iota((ens, LANES), 0)
    lane_id = iota((ens, LANES), 1)
    table = whole / (ens - 1) + as_float(row_id == lane_id)
    for i in range(ens):
        pivot_row = table[i : i + 1, :] / table[i : i + 1, i : i + 1]
        table = jnp.where(row_id == i, pivot_row, table - table[:, i : i + 1] * pivot_row)
    mixing = (
        table - jnp.mean(table, axis=0, keepdims=True) + as_float(row_id + ens == lane_id)
    )
    for m in range(ens):
        factors = [
            jnp.broadcast_to(mixing[j : j + 1, ens + m : ens + m + 1], (SUB, nz)) for j in range(ens)
        ]
        for r in range(width):
            for c in range(0, part, SUB):
                total = factors[0] * cols[0, r, pl.ds(c, SUB)]
                for j in range(1, ens):
                    total = total + factors[j] * cols[j, r, pl.ds(c, SUB)]
                out[m, r, pl.ds(c, SUB)] = total

    each(first, "wait_send", True)
    for d in range(1, n_mem):
        column(d).wait_send()
        share(d).wait_send()
    for d in range(1, n_space):
        sum_part(d).wait_send()

    @pl.loop(1, SWEEPS + 1)
    def _(k):
        for m in range(members):
            for h in range(PARTS):
                each(s_halo(k, m, h), "wait_send", True)

                @pl.when(k < SWEEPS)
                def _(m=m, h=h):
                    each(p_halo(k, m, h), "wait_send", True)


def body(
    log_perm,
    saturation,
    pressure_init,
    wells,
    well_rate,
    obs_index,
    obs_weight,
    obs_value,
    obs_var,
    noise,
):
    n_mem = lax.axis_size("mem")
    n_space = lax.axis_size("space")
    members, width, ny, nz = log_perm.shape
    ens = members * n_mem
    yl = ny // SUB
    part = ny // n_mem
    row_taps = obs_index.size // (width * n_space)
    operands = (
        log_perm,
        saturation,
        pressure_init,
        wells[None],
        well_rate[None],
        obs_index.T,
        obs_weight.T,
        obs_value[None],
        obs_var[None],
        noise,
    )
    vmem = pl.BlockSpec(memory_space=pltpu.VMEM)
    state = pltpu.VMEM((SWEEPS + 1, members, width + 2, yl + 2, SUB, nz), jnp.float32)
    dma = pltpu.SemaphoreType.DMA
    return pl.pallas_call(
        functools.partial(kernel, n_mem, n_space),
        out_shape=jax.ShapeDtypeStruct((ens, width, part, nz), jnp.float32),
        in_specs=[pl.BlockSpec(memory_space=pltpu.HBM)] * 10,
        out_specs=vmem,
        scratch_shapes=[
            *[pltpu.VMEM(a.shape, a.dtype) for a in operands],
            pltpu.VMEM((width, nz, row_taps), jnp.float32),
            pltpu.VMEM((width, ny, row_taps), jnp.float32),
            pltpu.VMEM((width, row_taps, LANES), jnp.float32),
            pltpu.VMEM((2 * SUB + 16, LANES), jnp.float32),
            dma((11,)),
            state,
            state,
            state,
            state,
            pltpu.VMEM((members, width + 2, yl, SUB, nz), jnp.float32),
            pltpu.VMEM((width, yl, SUB, nz), jnp.float32),
            pltpu.VMEM((2, members, ny, nz), jnp.float32),
            pltpu.VMEM((2, ny, nz), jnp.float32),
            pltpu.VMEM((2, ny, nz), jnp.float32),
            pltpu.VMEM((ens, width, part, nz), jnp.float32),
            pltpu.VMEM((n_mem, ens, LANES), jnp.float32),
            pltpu.VMEM((n_space, ens, LANES), jnp.float32),
            dma((2, 3)),
            dma((2, 3)),
            dma((SWEEPS + 1, members, PARTS, 2)),
            dma((SWEEPS + 1, members, PARTS, 2)),
            dma((SWEEPS + 1, members, PARTS, 2)),
            dma((SWEEPS + 1, members, PARTS, 2)),
            dma((n_mem,)),
            dma((n_mem,)),
            dma((n_mem,)),
            dma((n_mem,)),
            dma((n_space,)),
            dma((n_space,)),
        ],
        compiler_params=pltpu.CompilerParams(
            collective_id=0, has_side_effects=True, vmem_limit_bytes=48 * 1024 * 1024
        ),
    )(*operands)


def solution(mesh):
    placed = (
        P("mem", "space", None, None),
        P("space", None, None),
        P("space", None, None),
        P(),
        P(),
        P(),
        P(),
        P(),
        P(),
        P(),
    )
    return jax.shard_map(
        body, mesh=mesh, in_specs=placed, out_specs=P(None, "space", "mem", None), check_vma=False
    )
```

```python
import functools

import jax
import jax.numpy as jnp
from jax import lax
from jax.experimental import pallas as pl
from jax.experimental.pallas import tpu as pltpu
from jax.sharding import PartitionSpec as P

SWEEPS = 6
time_step = 0.1
inflation = 4.0

MESH = pl.DeviceIdType.MESH
HIGH = lax.Precision.HIGHEST
SUB = 8
LANES = 128
CHUNK = 4
PARTS = 2


def iota(shape, dim):
    return lax.broadcasted_iota(jnp.int32, shape, dim)


def as_float(cond):
    return jnp.where(cond, 1.0, 0.0).astype(jnp.float32)


def inverse_of(x):
    r = pl.reciprocal(x, approx=True)
    return r * (2.0 - x * r)


def split_dot(a, hot):
    rows = a.shape[0]
    high = a.astype(jnp.bfloat16).astype(jnp.float32)
    rest = a - high
    middle = rest.astype(jnp.bfloat16).astype(jnp.float32)
    terms = jnp.concatenate([high, middle, rest - middle], axis=0).astype(jnp.bfloat16)
    got = jnp.dot(terms, hot.astype(jnp.bfloat16), preferred_element_type=jnp.float32)
    return got[:rows] + got[rows : 2 * rows] + got[2 * rows :]


def kernel(
    n_mem,
    n_space,
    lp_in,
    sat_in,
    pre_in,
    wells_in,
    rate_in,
    oi_in,
    ow_in,
    ov_in,
    var_in,
    noise_in,
    out,
    lp,
    sat,
    pre,
    wells,
    rate,
    oi,
    ow,
    ov,
    var,
    noise,
    z_hot,
    y_hot,
    tap_sum,
    obs_own,
    local_sem,
    S,
    L,
    F,
    Q,
    half_perm,
    src,
    faces,
    picks,
    lp_ghost,
    sat_ghost,
    pre_ghost,
    cols,
    pred,
    gram,
    first_send,
    first_recv,
    s_send,
    s_recv,
    p_send,
    p_recv,
    col_send,
    col_recv,
    pred_send,
    pred_recv,
    gram_send,
    gram_recv,
):
    members, width, ny, nz = lp.shape
    yl = ny // SUB
    part = ny // n_mem
    ens = members * n_mem
    total_rows = width * n_space
    nobs = oi.shape[1]
    taps = oi.shape[0]
    per_row = nobs // total_rows
    row_taps = taps * per_row
    local_obs = per_row * width
    plane = ny * nz
    mem = lax.axis_index("mem")
    place = lax.axis_index("space")
    has_left = place > 0
    has_right = place < n_space - 1

    arrivals = [
        pltpu.make_async_copy(a, b, local_sem.at[i])
        for i, (a, b) in enumerate(
            [
                (pre_in, pre),
                (sat_in, sat),
                (lp_in, lp),
                (wells_in, wells),
                (rate_in, rate),
                (oi_in, oi),
                (ow_in, ow),
                (ov_in, ov),
                (var_in, var),
                (noise_in, noise),
                (
                    lp_in.at[:, :, pl.ds(pl.multiple_of(mem * part, part), part)],
                    cols.at[pl.ds(mem * members, members)],
                ),
            ]
        )
    ]
    for copy in arrivals:
        copy.start()

    barrier = pltpu.get_barrier_semaphore()
    for d in range(1, n_mem):
        pl.semaphore_signal(
            barrier, inc=1, device_id=(lax.rem(mem + d, n_mem), place), device_id_type=MESH
        )
    for d in range(1, n_space):
        pl.semaphore_signal(
            barrier, inc=1, device_id=(mem, lax.rem(place + d, n_space)), device_id_type=MESH
        )

    def clear(row, side):
        S[:, :, row] = jnp.zeros_like(S[:, :, row])
        Q[:, :, row] = jnp.zeros_like(Q[:, :, row])
        lp_ghost[side] = jnp.zeros_like(lp_ghost[side])
        sat_ghost[side] = jnp.zeros_like(sat_ghost[side])
        pre_ghost[side] = jnp.zeros_like(pre_ghost[side])

    @pl.when(jnp.logical_not(has_left))
    def _():
        clear(0, 0)

    @pl.when(jnp.logical_not(has_right))
    def _():
        clear(width + 1, 1)

    pl.semaphore_wait(barrier, n_mem - 1 + n_space - 1)

    def remote(a, b, send, recv, target):
        return pltpu.make_async_remote_copy(
            src_ref=a, dst_ref=b, send_sem=send, recv_sem=recv, device_id=target, device_id_type=MESH
        )

    right = (mem, lax.rem(place + 1, n_space))
    left = (mem, lax.rem(place + n_space - 1, n_space))

    def first(side):
        row = width - 1 if side == 0 else 0
        target = right if side == 0 else left
        pairs = [
            (pre_in.at[row], pre_ghost.at[side]),
            (sat_in.at[row], sat_ghost.at[side]),
            (lp_in.at[:, row], lp_ghost.at[side]),
        ]
        return [
            remote(a, b, first_send.at[side, i], first_recv.at[side, i], target)
            for i, (a, b) in enumerate(pairs)
        ]

    piece = yl // PARTS

    def halo(field, send, recv, k, m, h, side):
        a = width if side == 0 else 1
        b = 0 if side == 0 else width + 1
        rows = pl.ds(1 + h * piece, piece)
        return remote(
            field.at[k, m, a, rows],
            field.at[k, m, b, rows],
            send.at[k, m, h, side],
            recv.at[k, m, h, side],
            right if side == 0 else left,
        )

    def each(make, to_do, sending):
        for side in (0, 1):
            there = (has_right, has_left)[side if sending else 1 - side]

            @pl.when(there)
            def _(side=side):
                for copy in make(side):
                    getattr(copy, to_do)()

    each(first, "start", True)

    def column(d):
        peer = lax.rem(mem + d, n_mem)
        return remote(
            lp_in.at[:, :, pl.ds(pl.multiple_of(peer * part, part), part)],
            cols.at[pl.ds(mem * members, members)],
            col_send.at[d],
            col_recv.at[d],
            (peer, place),
        )

    for d in range(1, n_mem):
        column(d).start()
    for copy in arrivals:
        copy.wait()

    def strided(ref, lead, c):
        return ref[(*lead, pl.ds(c, SUB, stride=yl), slice(None))]

    def props(half, s):
        water = s * s
        dry = 1.0 - s
        total = water + dry * dry * 0.25
        return half * total, water * inverse_of(total)

    sub = iota((SUB, nz), 0)
    lane = iota((SUB, nz), 1)
    inner = as_float(lane < nz - 1)
    not_first = as_float(lane > 0)
    ends = as_float((lane == 0) | (lane == nz - 1))
    sub_first = sub == 0
    sub_last = sub == SUB - 1

    def pads(field, k, m, r):
        top = field[k, m, r, yl]
        field[k, m, r, 0] = jnp.where(sub_first, 0.0, pltpu.roll(top, 1, 0))
        bottom = field[k, m, r, 1]
        field[k, m, r, yl + 1] = jnp.where(sub_last, 0.0, pltpu.roll(bottom, SUB - 1, 0))

    @pl.loop(0, width)
    def _(r):
        for c in range(yl):
            s = strided(sat, (r,), c)
            press = strided(pre, (r,), c)
            for m in range(members):
                half = 0.5 * jnp.exp(strided(lp, (m, r), c))
                lam, frac = props(half, s)
                half_perm[m, r + 1, c] = half
                S[0, m, r + 1, c + 1] = s
                L[0, m, r + 1, c + 1] = lam
                F[0, m, r + 1, c + 1] = frac
                Q[0, m, r + 1, c + 1] = press
        for m in range(members):
            pads(L, 0, m, r + 1)
            pads(F, 0, m, r + 1)
            pads(Q, 0, m, r + 1)

    well = wells[...].astype(jnp.float32)
    well_x = jnp.floor((well + 0.5) * (1.0 / plane))
    rest = well - well_x * plane
    well_y = jnp.floor((rest + 0.5) * (1.0 / nz))
    well_z = rest - well_y * nz
    count = well.shape[1]

    def held_y(lanes):
        shape = (yl, SUB, lanes)
        return (iota(shape, 1) * yl + iota(shape, 0)).astype(jnp.float32).reshape(ny, lanes)

    at_z = as_float(iota((nz, count), 0).astype(jnp.float32) == well_z)
    at_y = held_y(count) == well_y
    for r in range(width):
        here = well_x == (place * width + r).astype(jnp.float32)
        at_row = jnp.where(at_y & here, rate[...], 0.0)
        field = lax.dot_general(
            at_row, at_z, (((1,), (1,)), ((), ())), precision=HIGH, preferred_element_type=jnp.float32
        )
        src[r] = field.reshape(yl, SUB, nz)

    def tables(r):
        x = place * width + r
        tap_lane = iota((1, row_taps), 1)
        select = as_float(iota((nobs, row_taps), 0) == x + total_rows * (tap_lane % per_row))
        both = jnp.concatenate([oi[...].astype(jnp.float32), ow[...]], axis=0)
        found = split_dot(both, select)
        own_tap = iota((taps, row_taps), 0) == tap_lane // per_row
        index = jnp.sum(jnp.where(own_tap, found[:taps], 0.0), axis=0, keepdims=True)
        weight = jnp.sum(jnp.where(own_tap, found[taps:], 0.0), axis=0, keepdims=True)
        rest = index - (x * plane).astype(jnp.float32)
        cell_y = jnp.floor((rest + 0.5) * (1.0 / nz))
        cell_z = rest - cell_y * nz
        z_hot[r] = as_float(iota((nz, row_taps), 0).astype(jnp.float32) == cell_z)
        y_hot[r] = jnp.where(held_y(row_taps) == cell_y, weight, 0.0)
        tap_sum[r] = as_float(
            iota((row_taps, LANES), 1) == r * per_row + iota((row_taps, 1), 0) % per_row
        )

    def own_data():
        lane = iota((1, LANES), 1)
        cell = place * width + lane // per_row + total_rows * (lane % per_row)
        select = as_float(iota((nobs, LANES), 0) == jnp.where(lane < local_obs, cell, -1))
        rows = [jnp.broadcast_to(ov[...], (SUB, nobs)), jnp.broadcast_to(var[...], (SUB, nobs))]
        pad = jnp.zeros((16 - ens % 16, nobs), jnp.float32)
        obs_own[...] = split_dot(jnp.concatenate(rows + [noise[...], pad], axis=0), select)

    def first_ghosts():
        each(first, "wait_recv", False)
        for side in (0, 1):
            row = 0 if side == 0 else width + 1
            there = as_float(has_left if side == 0 else has_right)
            for c in range(yl):
                s = strided(sat_ghost, (side,), c)
                p = strided(pre_ghost, (side,), c)
                for m in range(members):
                    half = 0.5 * there * jnp.exp(strided(lp_ghost, (side, m), c))
                    lam, frac = props(half, s)
                    half_perm[m, row, c] = half
                    L[0, m, row, c + 1] = lam
                    F[0, m, row, c + 1] = frac
                    Q[0, m, row, c + 1] = p

    def slab(field, k, m, r, c):
        return field[k, m, r, pl.ds(c, CHUNK + 2)]

    def face(k, m, r, mid):
        flux = (L[k, m, r, mid] + L[k, m, r + 1, mid]) * (Q[k, m, r, mid] - Q[k, m, r + 1, mid])
        return flux * jnp.where(flux > 0.0, F[k, m, r, mid], F[k, m, r + 1, mid])

    def saturate(k, m, r, lo, hi, new_below, new_above, keep):
        for c in range(lo, hi, CHUNK):
            mid = pl.ds(1 + c, CHUNK)
            lam_y, frac_y, press_y = slab(L, k, m, r, c), slab(F, k, m, r, c), slab(Q, k, m, r, c)
            lam, frac, press = lam_y[1:-1], frac_y[1:-1], press_y[1:-1]
            flux = (lam_y[:-1] + lam_y[1:]) * (press_y[:-1] - press_y[1:])
            along = flux * jnp.where(flux > 0.0, frac_y[:-1], frac_y[1:])
            outflow = along[1:] - along[:-1]
            here = pl.ds(c, CHUNK)
            below = face(k, m, r - 1, mid) if new_below else faces[m, r - 1, here]
            above = face(k, m, r, mid) if new_above else faces[m, r, here]
            if keep and new_below:
                faces[m, r - 1, here] = below
            if keep and new_above:
                faces[m, r, here] = above
            outflow = outflow + (above - below)
            lam_next = pltpu.roll(lam, nz - 1, 2)
            frac_next = pltpu.roll(frac, nz - 1, 2)
            press_next = pltpu.roll(press, nz - 1, 2)
            flux = (lam + lam_next) * inner * (press - press_next)
            along = flux * jnp.where(flux > 0.0, frac, frac_next)
            outflow = outflow + (along - pltpu.roll(along, 1, 2))
            outflow = outflow + ends * jnp.maximum(lam * press, 0.0) * frac
            source = src[r - 1, pl.ds(c, CHUNK)]
            water = jnp.maximum(source, 0.0) + jnp.minimum(source, 0.0) * frac
            s = jnp.clip(S[k, m, r, mid] + time_step * (water - outflow), 0.0, 1.0)
            lam, frac = props(half_perm[m, r, pl.ds(c, CHUNK)], s)
            S[k + 1, m, r, mid] = s
            L[k + 1, m, r, mid] = lam
            F[k + 1, m, r, mid] = frac

    def saturate_pads(k, m, r):
        pads(L, k + 1, m, r)
        pads(F, k + 1, m, r)

    def pressure(k, m, r, lo, hi):
        for c in range(lo, hi, CHUNK):
            mid = pl.ds(1 + c, CHUNK)
            lam_y, press_y = slab(L, k + 1, m, r, c), slab(Q, k, m, r, c)
            both_y = lam_y * press_y
            lam, press = lam_y[1:-1], press_y[1:-1]
            numer = press + src[r - 1, pl.ds(c, CHUNK)] + both_y[2:] + both_y[:-2]
            lam_sum = lam_y[2:] + lam_y[:-2]
            press_sum = press_y[2:] + press_y[:-2]
            others = [(L[k + 1, m, row, mid], Q[k, m, row, mid]) for row in (r - 1, r + 1)]
            others.append((pltpu.roll(lam, 1, 2) * not_first, pltpu.roll(press, 1, 2) * not_first))
            others.append((pltpu.roll(lam, nz - 1, 2) * inner, pltpu.roll(press, nz - 1, 2) * inner))
            for a, b in others:
                numer = numer + a * b
                lam_sum = lam_sum + a
                press_sum = press_sum + b
            Q[k + 1, m, r, mid] = (numer + lam * press_sum) * inverse_of(
                1.0 + 6.0 * lam + lam_sum
            )

    def pressure_pads(k, m, r):
        pads(Q, k + 1, m, r)

    def ghost_props(k, m, row, lo, hi):
        for c in range(lo, hi, CHUNK):
            mid = pl.ds(1 + c, CHUNK)
            lam, frac = props(half_perm[m, row, pl.ds(c, CHUNK)], S[k, m, row, mid])
            L[k, m, row, mid] = lam
            F[k, m, row, mid] = frac

    def s_halo(k, m, h):
        return lambda side: [halo(S, s_send, s_recv, k, m, h, side)]

    def p_halo(k, m, h):
        return lambda side: [halo(Q, p_send, p_recv, k, m, h, side)]

    def saturate_inside(k, m):
        saturate(k, m, 2, 0, yl, True, True, True)
        saturate_pads(k, m, 2)

        @pl.loop(3, width)
        def _(r):
            saturate(k, m, r, 0, yl, False, True, True)
            saturate_pads(k, m, r)

    def saturate_border(k, m, h):
        saturate(k, m, 1, h * piece, (h + 1) * piece, True, False, False)
        saturate(k, m, width, h * piece, (h + 1) * piece, False, True, False)
        if h == PARTS - 1:
            saturate_pads(k, m, 1)
            saturate_pads(k, m, width)

    def pressure_inside(k, m):
        @pl.loop(2, width)
        def _(r):
            pressure(k, m, r, 0, yl)
            pressure_pads(k, m, r)

    def pressure_border(k, m, h):
        @pl.loop(0, 2)
        def _(i):
            r = 1 + i * (width - 1)
            pressure(k, m, r, h * piece, (h + 1) * piece)
            if h == PARTS - 1:
                pressure_pads(k, m, r)

    def picked_rows(some):
        own = jnp.zeros((ens, LANES), jnp.float32)
        for r in some:
            found = jnp.zeros((ens, row_taps), jnp.float32)
            fields = Q[SWEEPS, :, r + 1, pl.ds(1, yl)].reshape(members * ny, nz)
            columns = split_dot(fields, z_hot[r])
            for m in range(members):
                picked = jnp.sum(columns[m * ny : (m + 1) * ny] * y_hot[r], axis=0, keepdims=True)
                found = jnp.where(iota((ens, row_taps), 0) == mem * members + m, picked, found)
            own = own + split_dot(found, tap_sum[r])
        return own

    halves = [(m, h) for m in range(members) for h in range(PARTS)]

    @pl.loop(0, SWEEPS)
    def _(k):
        for m in range(members):
            saturate_inside(k, m)

        @pl.when(k == 0)
        def _():
            first_ghosts()

        for m, h in halves:

            @pl.when(k > 0)
            def _(m=m, h=h):
                each(p_halo(k, m, h), "wait_recv", False)

            saturate_border(k, m, h)
            each(s_halo(k + 1, m, h), "start", True)
        for m in range(members):
            pressure_inside(k, m)

        @pl.when(k < width)
        def _():
            tables(k)

        @pl.when(k == SWEEPS - 1)
        def _():
            own_data()
            picks[...] = picked_rows(range(1, width - 1))

        for m, h in halves:
            each(s_halo(k + 1, m, h), "wait_recv", False)

            @pl.loop(0, 2)
            def _(i, m=m, h=h):
                ghost_props(k + 1, m, i * (width + 1), h * piece, (h + 1) * piece)

            pressure_border(k, m, h)

            @pl.when(k + 1 < SWEEPS)
            def _(m=m, h=h):
                each(p_halo(k + 1, m, h), "start", True)

    pred[mem] = picks[...] + picked_rows((0, width - 1))

    def share(d):
        return remote(
            pred.at[mem], pred.at[mem], pred_send.at[d], pred_recv.at[d], (lax.rem(mem + d, n_mem), place)
        )

    for d in range(1, n_mem):
        share(d).start()
    value_own, var_own = obs_own[:SUB], obs_own[SUB : 2 * SUB]
    noise_own = obs_own[2 * SUB : 2 * SUB + ens]
    scale = jnp.where(iota((ens, LANES), 1) < local_obs, inflation * var_own, 1.0)
    inverse = jnp.where(iota((ens, LANES), 1) < local_obs, 1.0 / scale, 0.0)
    target_obs = value_own + jnp.sqrt(inflation * var_own) * noise_own
    for d in range(1, n_mem):
        share(d).wait_recv()
    predicted = pred[0]
    for a in range(1, n_mem):
        predicted = predicted + pred[a]
    dev = predicted - jnp.mean(predicted, axis=0, keepdims=True)
    resid = target_obs - predicted
    both = jnp.concatenate([dev, resid, jnp.zeros((LANES - 2 * ens, LANES), jnp.float32)], axis=0)
    gram[place] = lax.dot_general(
        dev * inverse, both, (((1,), (1,)), ((), ())), precision=HIGH, preferred_element_type=jnp.float32
    )

    def sum_part(d):
        return remote(
            gram.at[place],
            gram.at[place],
            gram_send.at[d],
            gram_recv.at[d],
            (mem, lax.rem(place + d, n_space)),
        )

    for d in range(1, n_space):
        sum_part(d).start()
    each(first, "wait_send", True)
    for d in range(1, n_mem):
        column(d).wait_send()
        share(d).wait_send()

    @pl.loop(1, SWEEPS + 1)
    def _(k):
        for m in range(members):
            for h in range(PARTS):
                each(s_halo(k, m, h), "wait_send", True)

                @pl.when(k < SWEEPS)
                def _(m=m, h=h):
                    each(p_halo(k, m, h), "wait_send", True)
    for d in range(1, n_mem):
        column(d).wait_recv()
    for d in range(1, n_space):
        sum_part(d).wait_recv()
    for d in range(1, n_space):
        sum_part(d).wait_send()
    whole = gram[0]
    for a in range(1, n_space):
        whole = whole + gram[a]

    row_id = iota((ens, LANES), 0)
    lane_id = iota((ens, LANES), 1)
    table = whole / (ens - 1) + as_float(row_id == lane_id)
    for i in range(ens):
        pivot_row = table[i : i + 1, :] / table[i : i + 1, i : i + 1]
        table = jnp.where(row_id == i, pivot_row, table - table[:, i : i + 1] * pivot_row)
    mixing = (
        table - jnp.mean(table, axis=0, keepdims=True) + as_float(row_id + ens == lane_id)
    )
    for m in range(ens):
        factors = [
            jnp.broadcast_to(mixing[j : j + 1, ens + m : ens + m + 1], (SUB, nz)) for j in range(ens)
        ]
        for r in range(width):
            for c in range(0, part, SUB):
                total = factors[0] * cols[0, r, pl.ds(c, SUB)]
                for j in range(1, ens):
                    total = total + factors[j] * cols[j, r, pl.ds(c, SUB)]
                out[m, r, pl.ds(c, SUB)] = total


def body(
    log_perm,
    saturation,
    pressure_init,
    wells,
    well_rate,
    obs_index,
    obs_weight,
    obs_value,
    obs_var,
    noise,
):
    n_mem = lax.axis_size("mem")
    n_space = lax.axis_size("space")
    members, width, ny, nz = log_perm.shape
    ens = members * n_mem
    yl = ny // SUB
    part = ny // n_mem
    row_taps = obs_index.size // (width * n_space)
    operands = (
        log_perm,
        saturation,
        pressure_init,
        wells[None],
        well_rate[None],
        obs_index.T,
        obs_weight.T,
        obs_value[None],
        obs_var[None],
        noise,
    )
    vmem = pl.BlockSpec(memory_space=pltpu.VMEM)
    state = pltpu.VMEM((SWEEPS + 1, members, width + 2, yl + 2, SUB, nz), jnp.float32)
    dma = pltpu.SemaphoreType.DMA
    return pl.pallas_call(
        functools.partial(kernel, n_mem, n_space),
        out_shape=jax.ShapeDtypeStruct((ens, width, part, nz), jnp.float32),
        in_specs=[pl.BlockSpec(memory_space=pltpu.HBM)] * 10,
        out_specs=vmem,
        scratch_shapes=[
            *[pltpu.VMEM(a.shape, a.dtype) for a in operands],
            pltpu.VMEM((width, nz, row_taps), jnp.float32),
            pltpu.VMEM((width, ny, row_taps), jnp.float32),
            pltpu.VMEM((width, row_taps, LANES), jnp.float32),
            pltpu.VMEM((2 * SUB + 16, LANES), jnp.float32),
            dma((11,)),
            state,
            state,
            state,
            state,
            pltpu.VMEM((members, width + 2, yl, SUB, nz), jnp.float32),
            pltpu.VMEM((width, yl, SUB, nz), jnp.float32),
            pltpu.VMEM((members, width, yl, SUB, nz), jnp.float32),
            pltpu.VMEM((ens, LANES), jnp.float32),
            pltpu.VMEM((2, members, ny, nz), jnp.float32),
            pltpu.VMEM((2, ny, nz), jnp.float32),
            pltpu.VMEM((2, ny, nz), jnp.float32),
            pltpu.VMEM((ens, width, part, nz), jnp.float32),
            pltpu.VMEM((n_mem, ens, LANES), jnp.float32),
            pltpu.VMEM((n_space, ens, LANES), jnp.float32),
            dma((2, 3)),
            dma((2, 3)),
            dma((SWEEPS + 1, members, PARTS, 2)),
            dma((SWEEPS + 1, members, PARTS, 2)),
            dma((SWEEPS + 1, members, PARTS, 2)),
            dma((SWEEPS + 1, members, PARTS, 2)),
            dma((n_mem,)),
            dma((n_mem,)),
            dma((n_mem,)),
            dma((n_mem,)),
            dma((n_space,)),
            dma((n_space,)),
        ],
        compiler_params=pltpu.CompilerParams(
            collective_id=0, has_side_effects=True, vmem_limit_bytes=62 * 1024 * 1024
        ),
    )(*operands)


def solution(mesh):
    placed = (
        P("mem", "space", None, None),
        P("space", None, None),
        P("space", None, None),
        P(),
        P(),
        P(),
        P(),
        P(),
        P(),
        P(),
    )
    return jax.shard_map(
        body, mesh=mesh, in_specs=placed, out_specs=P(None, "space", "mem", None), check_vma=False
    )
```

```python
import functools

import jax
import jax.numpy as jnp
from jax import lax
from jax.experimental import pallas as pl
from jax.experimental.pallas import tpu as pltpu
from jax.sharding import PartitionSpec as P

SWEEPS = 6
time_step = 0.1
inflation = 4.0

MESH = pl.DeviceIdType.MESH
HIGH = lax.Precision.HIGHEST
SUB = 8
LANES = 128
CHUNK = 4
PARTS = 2


def iota(shape, dim):
    return lax.broadcasted_iota(jnp.int32, shape, dim)


def as_float(cond):
    return jnp.where(cond, 1.0, 0.0).astype(jnp.float32)


def inverse_of(x):
    r = pl.reciprocal(x, approx=True)
    return r * (2.0 - x * r)


def split_dot(a, hot):
    rows = a.shape[0]
    high = a.astype(jnp.bfloat16).astype(jnp.float32)
    rest = a - high
    middle = rest.astype(jnp.bfloat16).astype(jnp.float32)
    terms = jnp.concatenate([high, middle, rest - middle], axis=0).astype(jnp.bfloat16)
    got = jnp.dot(terms, hot.astype(jnp.bfloat16), preferred_element_type=jnp.float32)
    return got[:rows] + got[rows : 2 * rows] + got[2 * rows :]


def kernel(
    n_mem,
    n_space,
    lp_in,
    sat_in,
    pre_in,
    wells_in,
    rate_in,
    oi_in,
    ow_in,
    ov_in,
    var_in,
    noise_in,
    cols,
    mixing,
    lp,
    sat,
    pre,
    wells,
    rate,
    oi,
    ow,
    ov,
    var,
    noise,
    z_hot,
    y_hot,
    tap_sum,
    obs_own,
    local_sem,
    S,
    L,
    F,
    Q,
    half_perm,
    src,
    faces,
    picks,
    lp_ghost,
    sat_ghost,
    pre_ghost,
    pred,
    gram,
    first_send,
    first_recv,
    s_send,
    s_recv,
    p_send,
    p_recv,
    col_send,
    col_recv,
    pred_send,
    pred_recv,
    gram_send,
    gram_recv,
):
    members, width, ny, nz = lp.shape
    yl = ny // SUB
    part = ny // n_mem
    ens = members * n_mem
    total_rows = width * n_space
    nobs = oi.shape[1]
    taps = oi.shape[0]
    per_row = nobs // total_rows
    row_taps = taps * per_row
    local_obs = per_row * width
    plane = ny * nz
    mem = lax.axis_index("mem")
    place = lax.axis_index("space")
    has_left = place > 0
    has_right = place < n_space - 1

    arrivals = [
        pltpu.make_async_copy(a, b, local_sem.at[i])
        for i, (a, b) in enumerate(
            [
                (pre_in, pre),
                (sat_in, sat),
                (lp_in, lp),
                (wells_in, wells),
                (rate_in, rate),
                (oi_in, oi),
                (ow_in, ow),
                (ov_in, ov),
                (var_in, var),
                (noise_in, noise),
                (
                    lp_in.at[:, :, pl.ds(pl.multiple_of(mem * part, part), part)],
                    cols.at[pl.ds(mem * members, members)],
                ),
            ]
        )
    ]
    for copy in arrivals:
        copy.start()

    barrier = pltpu.get_barrier_semaphore()
    for d in range(1, n_mem):
        pl.semaphore_signal(
            barrier, inc=1, device_id=(lax.rem(mem + d, n_mem), place), device_id_type=MESH
        )
    for d in range(1, n_space):
        pl.semaphore_signal(
            barrier, inc=1, device_id=(mem, lax.rem(place + d, n_space)), device_id_type=MESH
        )

    def clear(row, side):
        S[:, :, row] = jnp.zeros_like(S[:, :, row])
        Q[:, :, row] = jnp.zeros_like(Q[:, :, row])
        lp_ghost[side] = jnp.zeros_like(lp_ghost[side])
        sat_ghost[side] = jnp.zeros_like(sat_ghost[side])
        pre_ghost[side] = jnp.zeros_like(pre_ghost[side])

    @pl.when(jnp.logical_not(has_left))
    def _():
        clear(0, 0)

    @pl.when(jnp.logical_not(has_right))
    def _():
        clear(width + 1, 1)

    pl.semaphore_wait(barrier, n_mem - 1 + n_space - 1)

    def remote(a, b, send, recv, target):
        return pltpu.make_async_remote_copy(
            src_ref=a, dst_ref=b, send_sem=send, recv_sem=recv, device_id=target, device_id_type=MESH
        )

    right = (mem, lax.rem(place + 1, n_space))
    left = (mem, lax.rem(place + n_space - 1, n_space))

    def first(side):
        row = width - 1 if side == 0 else 0
        target = right if side == 0 else left
        pairs = [
            (pre_in.at[row], pre_ghost.at[side]),
            (sat_in.at[row], sat_ghost.at[side]),
            (lp_in.at[:, row], lp_ghost.at[side]),
        ]
        return [
            remote(a, b, first_send.at[side, i], first_recv.at[side, i], target)
            for i, (a, b) in enumerate(pairs)
        ]

    piece = yl // PARTS

    def halo(field, send, recv, k, m, h, side):
        a = width if side == 0 else 1
        b = 0 if side == 0 else width + 1
        rows = pl.ds(1 + h * piece, piece)
        return remote(
            field.at[k, m, a, rows],
            field.at[k, m, b, rows],
            send.at[k, m, h, side],
            recv.at[k, m, h, side],
            right if side == 0 else left,
        )

    def each(make, to_do, sending):
        for side in (0, 1):
            there = (has_right, has_left)[side if sending else 1 - side]

            @pl.when(there)
            def _(side=side):
                for copy in make(side):
                    getattr(copy, to_do)()

    each(first, "start", True)

    def column(d):
        peer = lax.rem(mem + d, n_mem)
        return remote(
            lp_in.at[:, :, pl.ds(pl.multiple_of(peer * part, part), part)],
            cols.at[pl.ds(mem * members, members)],
            col_send.at[d],
            col_recv.at[d],
            (peer, place),
        )

    for d in range(1, n_mem):
        column(d).start()
    for copy in arrivals:
        copy.wait()

    def strided(ref, lead, c):
        return ref[(*lead, pl.ds(c, SUB, stride=yl), slice(None))]

    def props(half, s):
        water = s * s
        dry = 1.0 - s
        total = water + dry * dry * 0.25
        return half * total, water * inverse_of(total)

    sub = iota((SUB, nz), 0)
    lane = iota((SUB, nz), 1)
    inner = as_float(lane < nz - 1)
    not_first = as_float(lane > 0)
    ends = as_float((lane == 0) | (lane == nz - 1))
    sub_first = sub == 0
    sub_last = sub == SUB - 1

    def pads(field, k, m, r):
        top = field[k, m, r, yl]
        field[k, m, r, 0] = jnp.where(sub_first, 0.0, pltpu.roll(top, 1, 0))
        bottom = field[k, m, r, 1]
        field[k, m, r, yl + 1] = jnp.where(sub_last, 0.0, pltpu.roll(bottom, SUB - 1, 0))

    @pl.loop(0, width)
    def _(r):
        for c in range(yl):
            s = strided(sat, (r,), c)
            press = strided(pre, (r,), c)
            for m in range(members):
                half = 0.5 * jnp.exp(strided(lp, (m, r), c))
                lam, frac = props(half, s)
                half_perm[m, r + 1, c] = half
                S[0, m, r + 1, c + 1] = s
                L[0, m, r + 1, c + 1] = lam
                F[0, m, r + 1, c + 1] = frac
                Q[0, m, r + 1, c + 1] = press
        for m in range(members):
            pads(L, 0, m, r + 1)
            pads(F, 0, m, r + 1)
            pads(Q, 0, m, r + 1)

    well = wells[...].astype(jnp.float32)
    well_x = jnp.floor((well + 0.5) * (1.0 / plane))
    rest = well - well_x * plane
    well_y = jnp.floor((rest + 0.5) * (1.0 / nz))
    well_z = rest - well_y * nz
    count = well.shape[1]

    def held_y(lanes):
        shape = (yl, SUB, lanes)
        return (iota(shape, 1) * yl + iota(shape, 0)).astype(jnp.float32).reshape(ny, lanes)

    at_z = as_float(iota((nz, count), 0).astype(jnp.float32) == well_z)
    at_y = held_y(count) == well_y
    for r in range(width):
        here = well_x == (place * width + r).astype(jnp.float32)
        at_row = jnp.where(at_y & here, rate[...], 0.0)
        field = lax.dot_general(
            at_row, at_z, (((1,), (1,)), ((), ())), precision=HIGH, preferred_element_type=jnp.float32
        )
        src[r] = field.reshape(yl, SUB, nz)

    def tables(r):
        x = place * width + r
        tap_lane = iota((1, row_taps), 1)
        select = as_float(iota((nobs, row_taps), 0) == x + total_rows * (tap_lane % per_row))
        both = jnp.concatenate([oi[...].astype(jnp.float32), ow[...]], axis=0)
        found = split_dot(both, select)
        own_tap = iota((taps, row_taps), 0) == tap_lane // per_row
        index = jnp.sum(jnp.where(own_tap, found[:taps], 0.0), axis=0, keepdims=True)
        weight = jnp.sum(jnp.where(own_tap, found[taps:], 0.0), axis=0, keepdims=True)
        rest = index - (x * plane).astype(jnp.float32)
        cell_y = jnp.floor((rest + 0.5) * (1.0 / nz))
        cell_z = rest - cell_y * nz
        z_hot[r] = as_float(iota((nz, row_taps), 0).astype(jnp.float32) == cell_z)
        y_hot[r] = jnp.where(held_y(row_taps) == cell_y, weight, 0.0)
        tap_sum[r] = as_float(
            iota((row_taps, LANES), 1) == r * per_row + iota((row_taps, 1), 0) % per_row
        )

    def own_data():
        lane = iota((1, LANES), 1)
        cell = place * width + lane // per_row + total_rows * (lane % per_row)
        select = as_float(iota((nobs, LANES), 0) == jnp.where(lane < local_obs, cell, -1))
        rows = [jnp.broadcast_to(ov[...], (SUB, nobs)), jnp.broadcast_to(var[...], (SUB, nobs))]
        pad = jnp.zeros((16 - ens % 16, nobs), jnp.float32)
        obs_own[...] = split_dot(jnp.concatenate(rows + [noise[...], pad], axis=0), select)

    def first_ghosts():
        each(first, "wait_recv", False)
        for side in (0, 1):
            row = 0 if side == 0 else width + 1
            there = as_float(has_left if side == 0 else has_right)
            for c in range(yl):
                s = strided(sat_ghost, (side,), c)
                p = strided(pre_ghost, (side,), c)
                for m in range(members):
                    half = 0.5 * there * jnp.exp(strided(lp_ghost, (side, m), c))
                    lam, frac = props(half, s)
                    half_perm[m, row, c] = half
                    L[0, m, row, c + 1] = lam
                    F[0, m, row, c + 1] = frac
                    Q[0, m, row, c + 1] = p

    def slab(field, k, m, r, c):
        return field[k, m, r, pl.ds(c, CHUNK + 2)]

    def face(k, m, r, mid):
        flux = (L[k, m, r, mid] + L[k, m, r + 1, mid]) * (Q[k, m, r, mid] - Q[k, m, r + 1, mid])
        return flux * jnp.where(flux > 0.0, F[k, m, r, mid], F[k, m, r + 1, mid])

    def saturate(k, m, r, lo, hi, new_below, new_above, keep):
        for c in range(lo, hi, CHUNK):
            mid = pl.ds(1 + c, CHUNK)
            lam_y, frac_y, press_y = slab(L, k, m, r, c), slab(F, k, m, r, c), slab(Q, k, m, r, c)
            lam, frac, press = lam_y[1:-1], frac_y[1:-1], press_y[1:-1]
            flux = (lam_y[:-1] + lam_y[1:]) * (press_y[:-1] - press_y[1:])
            along = flux * jnp.where(flux > 0.0, frac_y[:-1], frac_y[1:])
            outflow = along[1:] - along[:-1]
            here = pl.ds(c, CHUNK)
            below = face(k, m, r - 1, mid) if new_below else faces[m, r - 1, here]
            above = face(k, m, r, mid) if new_above else faces[m, r, here]
            if keep and new_below:
                faces[m, r - 1, here] = below
            if keep and new_above:
                faces[m, r, here] = above
            outflow = outflow + (above - below)
            lam_next = pltpu.roll(lam, nz - 1, 2)
            frac_next = pltpu.roll(frac, nz - 1, 2)
            press_next = pltpu.roll(press, nz - 1, 2)
            flux = (lam + lam_next) * inner * (press - press_next)
            along = flux * jnp.where(flux > 0.0, frac, frac_next)
            outflow = outflow + (along - pltpu.roll(along, 1, 2))
            outflow = outflow + ends * jnp.maximum(lam * press, 0.0) * frac
            source = src[r - 1, pl.ds(c, CHUNK)]
            water = jnp.maximum(source, 0.0) + jnp.minimum(source, 0.0) * frac
            s = jnp.clip(S[k, m, r, mid] + time_step * (water - outflow), 0.0, 1.0)
            lam, frac = props(half_perm[m, r, pl.ds(c, CHUNK)], s)
            S[k + 1, m, r, mid] = s
            L[k + 1, m, r, mid] = lam
            F[k + 1, m, r, mid] = frac

    def saturate_pads(k, m, r):
        pads(L, k + 1, m, r)
        pads(F, k + 1, m, r)

    def pressure(k, m, r, lo, hi):
        for c in range(lo, hi, CHUNK):
            mid = pl.ds(1 + c, CHUNK)
            lam_y, press_y = slab(L, k + 1, m, r, c), slab(Q, k, m, r, c)
            both_y = lam_y * press_y
            lam, press = lam_y[1:-1], press_y[1:-1]
            numer = press + src[r - 1, pl.ds(c, CHUNK)] + both_y[2:] + both_y[:-2]
            lam_sum = lam_y[2:] + lam_y[:-2]
            press_sum = press_y[2:] + press_y[:-2]
            others = [(L[k + 1, m, row, mid], Q[k, m, row, mid]) for row in (r - 1, r + 1)]
            others.append((pltpu.roll(lam, 1, 2) * not_first, pltpu.roll(press, 1, 2) * not_first))
            others.append((pltpu.roll(lam, nz - 1, 2) * inner, pltpu.roll(press, nz - 1, 2) * inner))
            for a, b in others:
                numer = numer + a * b
                lam_sum = lam_sum + a
                press_sum = press_sum + b
            Q[k + 1, m, r, mid] = (numer + lam * press_sum) * inverse_of(
                1.0 + 6.0 * lam + lam_sum
            )

    def pressure_pads(k, m, r):
        pads(Q, k + 1, m, r)

    def ghost_props(k, m, row, lo, hi):
        for c in range(lo, hi, CHUNK):
            mid = pl.ds(1 + c, CHUNK)
            lam, frac = props(half_perm[m, row, pl.ds(c, CHUNK)], S[k, m, row, mid])
            L[k, m, row, mid] = lam
            F[k, m, row, mid] = frac

    def s_halo(k, m, h):
        return lambda side: [halo(S, s_send, s_recv, k, m, h, side)]

    def p_halo(k, m, h):
        return lambda side: [halo(Q, p_send, p_recv, k, m, h, side)]

    def saturate_inside(k, m):
        saturate(k, m, 2, 0, yl, True, True, True)
        saturate_pads(k, m, 2)

        @pl.loop(3, width)
        def _(r):
            saturate(k, m, r, 0, yl, False, True, True)
            saturate_pads(k, m, r)

    def saturate_border(k, m, h):
        saturate(k, m, 1, h * piece, (h + 1) * piece, True, False, False)
        saturate(k, m, width, h * piece, (h + 1) * piece, False, True, False)
        if h == PARTS - 1:
            saturate_pads(k, m, 1)
            saturate_pads(k, m, width)

    def pressure_inside(k, m):
        @pl.loop(2, width)
        def _(r):
            pressure(k, m, r, 0, yl)
            pressure_pads(k, m, r)

    def pressure_border(k, m, h):
        @pl.loop(0, 2)
        def _(i):
            r = 1 + i * (width - 1)
            pressure(k, m, r, h * piece, (h + 1) * piece)
            if h == PARTS - 1:
                pressure_pads(k, m, r)

    def picked_rows(some):
        own = jnp.zeros((ens, LANES), jnp.float32)
        for r in some:
            found = jnp.zeros((ens, row_taps), jnp.float32)
            fields = Q[SWEEPS, :, r + 1, pl.ds(1, yl)].reshape(members * ny, nz)
            columns = split_dot(fields, z_hot[r])
            for m in range(members):
                picked = jnp.sum(columns[m * ny : (m + 1) * ny] * y_hot[r], axis=0, keepdims=True)
                found = jnp.where(iota((ens, row_taps), 0) == mem * members + m, picked, found)
            own = own + split_dot(found, tap_sum[r])
        return own

    for m in range(members):
        saturate_inside(0, m)
    first_ghosts()

    @pl.loop(0, SWEEPS)
    def _(k):
        for m in range(members):
            for h in range(PARTS):

                @pl.when(k > 0)
                def _(m=m, h=h):
                    each(p_halo(k, m, h), "wait_recv", False)

                saturate_border(k, m, h)
                each(s_halo(k + 1, m, h), "start", True)
            pressure_inside(k, m)

        @pl.when(k < width)
        def _():
            tables(k)

        @pl.when(k == SWEEPS - 1)
        def _():
            own_data()
            picks[...] = picked_rows(range(1, width - 1))

        for m in range(members):
            for h in range(PARTS):
                each(s_halo(k + 1, m, h), "wait_recv", False)

                @pl.loop(0, 2)
                def _(i, m=m, h=h):
                    ghost_props(k + 1, m, i * (width + 1), h * piece, (h + 1) * piece)

                pressure_border(k, m, h)

                @pl.when(k + 1 < SWEEPS)
                def _(m=m, h=h):
                    each(p_halo(k + 1, m, h), "start", True)

            @pl.when(k + 1 < SWEEPS)
            def _(m=m):
                saturate_inside(k + 1, m)

    pred[mem] = picks[...] + picked_rows((0, width - 1))

    def share(d):
        return remote(
            pred.at[mem], pred.at[mem], pred_send.at[d], pred_recv.at[d], (lax.rem(mem + d, n_mem), place)
        )

    for d in range(1, n_mem):
        share(d).start()
    value_own, var_own = obs_own[:SUB], obs_own[SUB : 2 * SUB]
    noise_own = obs_own[2 * SUB : 2 * SUB + ens]
    scale = jnp.where(iota((ens, LANES), 1) < local_obs, inflation * var_own, 1.0)
    inverse = jnp.where(iota((ens, LANES), 1) < local_obs, 1.0 / scale, 0.0)
    target_obs = value_own + jnp.sqrt(inflation * var_own) * noise_own
    for d in range(1, n_mem):
        share(d).wait_recv()
    predicted = pred[0]
    for a in range(1, n_mem):
        predicted = predicted + pred[a]
    dev = predicted - jnp.mean(predicted, axis=0, keepdims=True)
    resid = target_obs - predicted
    both = jnp.concatenate([dev, resid, jnp.zeros((LANES - 2 * ens, LANES), jnp.float32)], axis=0)
    gram[place] = lax.dot_general(
        dev * inverse, both, (((1,), (1,)), ((), ())), precision=HIGH, preferred_element_type=jnp.float32
    )

    def sum_part(d):
        return remote(
            gram.at[place],
            gram.at[place],
            gram_send.at[d],
            gram_recv.at[d],
            (mem, lax.rem(place + d, n_space)),
        )

    for d in range(1, n_space):
        sum_part(d).start()
    each(first, "wait_send", True)
    for d in range(1, n_mem):
        column(d).wait_send()
        share(d).wait_send()

    @pl.loop(1, SWEEPS + 1)
    def _(k):
        for m in range(members):
            for h in range(PARTS):
                each(s_halo(k, m, h), "wait_send", True)

                @pl.when(k < SWEEPS)
                def _(m=m, h=h):
                    each(p_halo(k, m, h), "wait_send", True)
    for d in range(1, n_mem):
        column(d).wait_recv()
    for d in range(1, n_space):
        sum_part(d).wait_recv()
    for d in range(1, n_space):
        sum_part(d).wait_send()
    whole = gram[0]
    for a in range(1, n_space):
        whole = whole + gram[a]

    row_id = iota((ens, LANES), 0)
    lane_id = iota((ens, LANES), 1)
    table = whole / (ens - 1) + as_float(row_id == lane_id)
    for i in range(ens):
        pivot_row = table[i : i + 1, :] / table[i : i + 1, i : i + 1]
        table = jnp.where(row_id == i, pivot_row, table - table[:, i : i + 1] * pivot_row)
    mixing[...] = (
        table - jnp.mean(table, axis=0, keepdims=True) + as_float(row_id + ens == lane_id)
    )


def mix_kernel(mixing, cols, out):
    ens, _, part, nz = cols.shape
    factors = [
        [
            jnp.broadcast_to(mixing[j : j + 1, ens + m : ens + m + 1], (SUB, nz))
            for j in range(ens)
        ]
        for m in range(ens)
    ]
    for c in range(0, part, SUB):
        rows = [cols[j, 0, pl.ds(c, SUB)] for j in range(ens)]
        for m in range(ens):
            total = factors[m][0] * rows[0]
            for j in range(1, ens):
                total = total + factors[m][j] * rows[j]
            out[m, 0, pl.ds(c, SUB)] = total


def body(
    log_perm,
    saturation,
    pressure_init,
    wells,
    well_rate,
    obs_index,
    obs_weight,
    obs_value,
    obs_var,
    noise,
):
    n_mem = lax.axis_size("mem")
    n_space = lax.axis_size("space")
    members, width, ny, nz = log_perm.shape
    ens = members * n_mem
    yl = ny // SUB
    part = ny // n_mem
    row_taps = obs_index.size // (width * n_space)
    operands = (
        log_perm,
        saturation,
        pressure_init,
        wells[None],
        well_rate[None],
        obs_index.T,
        obs_weight.T,
        obs_value[None],
        obs_var[None],
        noise,
    )
    vmem = pl.BlockSpec(memory_space=pltpu.VMEM)
    state = pltpu.VMEM((SWEEPS + 1, members, width + 2, yl + 2, SUB, nz), jnp.float32)
    dma = pltpu.SemaphoreType.DMA
    columns = jax.ShapeDtypeStruct((ens, width, part, nz), jnp.float32)
    cols, mixing = pl.pallas_call(
        functools.partial(kernel, n_mem, n_space),
        out_shape=(columns, jax.ShapeDtypeStruct((ens, LANES), jnp.float32)),
        in_specs=[pl.BlockSpec(memory_space=pltpu.HBM)] * 10,
        out_specs=(pl.BlockSpec(memory_space=pltpu.HBM), vmem),
        scratch_shapes=[
            *[pltpu.VMEM(a.shape, a.dtype) for a in operands],
            pltpu.VMEM((width, nz, row_taps), jnp.float32),
            pltpu.VMEM((width, ny, row_taps), jnp.float32),
            pltpu.VMEM((width, row_taps, LANES), jnp.float32),
            pltpu.VMEM((2 * SUB + 16, LANES), jnp.float32),
            dma((11,)),
            state,
            state,
            state,
            state,
            pltpu.VMEM((members, width + 2, yl, SUB, nz), jnp.float32),
            pltpu.VMEM((width, yl, SUB, nz), jnp.float32),
            pltpu.VMEM((members, width, yl, SUB, nz), jnp.float32),
            pltpu.VMEM((ens, LANES), jnp.float32),
            pltpu.VMEM((2, members, ny, nz), jnp.float32),
            pltpu.VMEM((2, ny, nz), jnp.float32),
            pltpu.VMEM((2, ny, nz), jnp.float32),
            pltpu.VMEM((n_mem, ens, LANES), jnp.float32),
            pltpu.VMEM((n_space, ens, LANES), jnp.float32),
            dma((2, 3)),
            dma((2, 3)),
            dma((SWEEPS + 1, members, PARTS, 2)),
            dma((SWEEPS + 1, members, PARTS, 2)),
            dma((SWEEPS + 1, members, PARTS, 2)),
            dma((SWEEPS + 1, members, PARTS, 2)),
            dma((n_mem,)),
            dma((n_mem,)),
            dma((n_mem,)),
            dma((n_mem,)),
            dma((n_space,)),
            dma((n_space,)),
        ],
        compiler_params=pltpu.CompilerParams(
            collective_id=0, has_side_effects=True, vmem_limit_bytes=62 * 1024 * 1024
        ),
    )(*operands)
    block = pl.BlockSpec((ens, 1, part, nz), lambda r: (0, r, 0, 0))
    return pl.pallas_call(
        mix_kernel,
        grid=(width,),
        out_shape=columns,
        in_specs=[pl.BlockSpec((ens, LANES), lambda r: (0, 0)), block],
        out_specs=block,
        compiler_params=pltpu.CompilerParams(vmem_limit_bytes=62 * 1024 * 1024),
    )(mixing, cols)


def solution(mesh):
    placed = (
        P("mem", "space", None, None),
        P("space", None, None),
        P("space", None, None),
        P(),
        P(),
        P(),
        P(),
        P(),
        P(),
        P(),
    )
    return jax.shard_map(
        body, mesh=mesh, in_specs=placed, out_specs=P(None, "space", "mem", None), check_vma=False
    )
```

```python
import functools

import jax
import jax.numpy as jnp
from jax import lax
from jax.experimental import pallas as pl
from jax.experimental.pallas import tpu as pltpu
from jax.sharding import PartitionSpec as P

SWEEPS = 6
time_step = 0.1
inflation = 4.0

MESH = pl.DeviceIdType.MESH
HIGH = lax.Precision.HIGHEST
SUB = 8
LANES = 128
CHUNK = 8
PARTS = 1


def iota(shape, dim):
    return lax.broadcasted_iota(jnp.int32, shape, dim)


def as_float(cond):
    return jnp.where(cond, 1.0, 0.0).astype(jnp.float32)


def inverse_of(x):
    r = pl.reciprocal(x, approx=True)
    return r * (2.0 - x * r)


def split_dot(a, hot):
    rows = a.shape[0]
    high = a.astype(jnp.bfloat16).astype(jnp.float32)
    rest = a - high
    middle = rest.astype(jnp.bfloat16).astype(jnp.float32)
    terms = jnp.concatenate([high, middle, rest - middle], axis=0).astype(jnp.bfloat16)
    got = jnp.dot(terms, hot.astype(jnp.bfloat16), preferred_element_type=jnp.float32)
    return got[:rows] + got[rows : 2 * rows] + got[2 * rows :]


def kernel(
    n_mem,
    n_space,
    lp_in,
    sat_in,
    pre_in,
    wells_in,
    rate_in,
    oi_in,
    ow_in,
    ov_in,
    var_in,
    noise_in,
    out,
    lp,
    sat,
    pre,
    wells,
    rate,
    oi,
    ow,
    ov,
    var,
    noise,
    z_hot,
    y_hot,
    tap_sum,
    obs_own,
    local_sem,
    S,
    L,
    F,
    Q,
    half_perm,
    src,
    faces,
    picks,
    lp_ghost,
    sat_ghost,
    pre_ghost,
    cols,
    pred,
    gram,
    first_send,
    first_recv,
    s_send,
    s_recv,
    p_send,
    p_recv,
    col_send,
    col_recv,
    pred_send,
    pred_recv,
    gram_send,
    gram_recv,
):
    members, width, ny, nz = lp.shape
    yl = ny // SUB
    part = ny // n_mem
    ens = members * n_mem
    total_rows = width * n_space
    nobs = oi.shape[1]
    taps = oi.shape[0]
    per_row = nobs // total_rows
    row_taps = taps * per_row
    local_obs = per_row * width
    plane = ny * nz
    mem = lax.axis_index("mem")
    place = lax.axis_index("space")
    has_left = place > 0
    has_right = place < n_space - 1

    arrivals = [
        pltpu.make_async_copy(a, b, local_sem.at[i])
        for i, (a, b) in enumerate(
            [
                (pre_in, pre),
                (sat_in, sat),
                (lp_in, lp),
                (wells_in, wells),
                (rate_in, rate),
                (oi_in, oi),
                (ow_in, ow),
                (ov_in, ov),
                (var_in, var),
                (noise_in, noise),
                (
                    lp_in.at[:, :, pl.ds(pl.multiple_of(mem * part, part), part)],
                    cols.at[pl.ds(mem * members, members)],
                ),
            ]
        )
    ]
    for copy in arrivals:
        copy.start()

    barrier = pltpu.get_barrier_semaphore()
    for d in range(1, n_mem):
        pl.semaphore_signal(
            barrier, inc=1, device_id=(lax.rem(mem + d, n_mem), place), device_id_type=MESH
        )
    for d in range(1, n_space):
        pl.semaphore_signal(
            barrier, inc=1, device_id=(mem, lax.rem(place + d, n_space)), device_id_type=MESH
        )

    def clear(row, side):
        S[:, :, row] = jnp.zeros_like(S[:, :, row])
        Q[:, :, row] = jnp.zeros_like(Q[:, :, row])
        lp_ghost[side] = jnp.zeros_like(lp_ghost[side])
        sat_ghost[side] = jnp.zeros_like(sat_ghost[side])
        pre_ghost[side] = jnp.zeros_like(pre_ghost[side])

    @pl.when(jnp.logical_not(has_left))
    def _():
        clear(0, 0)

    @pl.when(jnp.logical_not(has_right))
    def _():
        clear(width + 1, 1)

    pl.semaphore_wait(barrier, n_mem - 1 + n_space - 1)

    def remote(a, b, send, recv, target):
        return pltpu.make_async_remote_copy(
            src_ref=a, dst_ref=b, send_sem=send, recv_sem=recv, device_id=target, device_id_type=MESH
        )

    right = (mem, lax.rem(place + 1, n_space))
    left = (mem, lax.rem(place + n_space - 1, n_space))

    def first(side):
        row = width - 1 if side == 0 else 0
        target = right if side == 0 else left
        pairs = [
            (pre_in.at[row], pre_ghost.at[side]),
            (sat_in.at[row], sat_ghost.at[side]),
            (lp_in.at[:, row], lp_ghost.at[side]),
        ]
        return [
            remote(a, b, first_send.at[side, i], first_recv.at[side, i], target)
            for i, (a, b) in enumerate(pairs)
        ]

    piece = yl // PARTS

    def halo(field, send, recv, k, m, h, side):
        a = width if side == 0 else 1
        b = 0 if side == 0 else width + 1
        rows = pl.ds(1 + h * piece, piece)
        return remote(
            field.at[k, m, a, rows],
            field.at[k, m, b, rows],
            send.at[k, m, h, side],
            recv.at[k, m, h, side],
            right if side == 0 else left,
        )

    def each(make, to_do, sending):
        for side in (0, 1):
            there = (has_right, has_left)[side if sending else 1 - side]

            @pl.when(there)
            def _(side=side):
                for copy in make(side):
                    getattr(copy, to_do)()

    each(first, "start", True)

    def column(d):
        peer = lax.rem(mem + d, n_mem)
        return remote(
            lp_in.at[:, :, pl.ds(pl.multiple_of(peer * part, part), part)],
            cols.at[pl.ds(mem * members, members)],
            col_send.at[d],
            col_recv.at[d],
            (peer, place),
        )

    for d in range(1, n_mem):
        column(d).start()
    for copy in arrivals:
        copy.wait()

    def strided(ref, lead, c):
        return ref[(*lead, pl.ds(c, SUB, stride=yl), slice(None))]

    def props(half, s):
        water = s * s
        dry = 1.0 - s
        total = water + dry * dry * 0.25
        return half * total, water * inverse_of(total)

    sub = iota((SUB, nz), 0)
    lane = iota((SUB, nz), 1)
    inner = as_float(lane < nz - 1)
    not_first = as_float(lane > 0)
    ends = as_float((lane == 0) | (lane == nz - 1))
    sub_first = sub == 0
    sub_last = sub == SUB - 1

    def pads(field, k, m, r):
        top = field[k, m, r, yl]
        field[k, m, r, 0] = jnp.where(sub_first, 0.0, pltpu.roll(top, 1, 0))
        bottom = field[k, m, r, 1]
        field[k, m, r, yl + 1] = jnp.where(sub_last, 0.0, pltpu.roll(bottom, SUB - 1, 0))

    @pl.loop(0, width)
    def _(r):
        for c in range(yl):
            s = strided(sat, (r,), c)
            press = strided(pre, (r,), c)
            for m in range(members):
                half = 0.5 * jnp.exp(strided(lp, (m, r), c))
                lam, frac = props(half, s)
                half_perm[m, r + 1, c] = half
                S[0, m, r + 1, c + 1] = s
                L[0, m, r + 1, c + 1] = lam
                F[0, m, r + 1, c + 1] = frac
                Q[0, m, r + 1, c + 1] = press
        for m in range(members):
            pads(L, 0, m, r + 1)
            pads(F, 0, m, r + 1)
            pads(Q, 0, m, r + 1)

    well = wells[...].astype(jnp.float32)
    well_x = jnp.floor((well + 0.5) * (1.0 / plane))
    rest = well - well_x * plane
    well_y = jnp.floor((rest + 0.5) * (1.0 / nz))
    well_z = rest - well_y * nz
    count = well.shape[1]

    def held_y(lanes):
        shape = (yl, SUB, lanes)
        return (iota(shape, 1) * yl + iota(shape, 0)).astype(jnp.float32).reshape(ny, lanes)

    at_z = as_float(iota((nz, count), 0).astype(jnp.float32) == well_z)
    at_y = held_y(count) == well_y
    for r in range(width):
        here = well_x == (place * width + r).astype(jnp.float32)
        at_row = jnp.where(at_y & here, rate[...], 0.0)
        field = lax.dot_general(
            at_row, at_z, (((1,), (1,)), ((), ())), precision=HIGH, preferred_element_type=jnp.float32
        )
        src[r] = field.reshape(yl, SUB, nz)

    def tables(r):
        x = place * width + r
        tap_lane = iota((1, row_taps), 1)
        select = as_float(iota((nobs, row_taps), 0) == x + total_rows * (tap_lane % per_row))
        both = jnp.concatenate([oi[...].astype(jnp.float32), ow[...]], axis=0)
        found = split_dot(both, select)
        own_tap = iota((taps, row_taps), 0) == tap_lane // per_row
        index = jnp.sum(jnp.where(own_tap, found[:taps], 0.0), axis=0, keepdims=True)
        weight = jnp.sum(jnp.where(own_tap, found[taps:], 0.0), axis=0, keepdims=True)
        rest = index - (x * plane).astype(jnp.float32)
        cell_y = jnp.floor((rest + 0.5) * (1.0 / nz))
        cell_z = rest - cell_y * nz
        z_hot[r] = as_float(iota((nz, row_taps), 0).astype(jnp.float32) == cell_z)
        y_hot[r] = jnp.where(held_y(row_taps) == cell_y, weight, 0.0)
        tap_sum[r] = as_float(
            iota((row_taps, LANES), 1) == r * per_row + iota((row_taps, 1), 0) % per_row
        )

    def own_data():
        lane = iota((1, LANES), 1)
        cell = place * width + lane // per_row + total_rows * (lane % per_row)
        select = as_float(iota((nobs, LANES), 0) == jnp.where(lane < local_obs, cell, -1))
        rows = [jnp.broadcast_to(ov[...], (SUB, nobs)), jnp.broadcast_to(var[...], (SUB, nobs))]
        pad = jnp.zeros((16 - ens % 16, nobs), jnp.float32)
        obs_own[...] = split_dot(jnp.concatenate(rows + [noise[...], pad], axis=0), select)

    def first_ghosts():
        each(first, "wait_recv", False)
        for side in (0, 1):
            row = 0 if side == 0 else width + 1
            there = as_float(has_left if side == 0 else has_right)
            for c in range(yl):
                s = strided(sat_ghost, (side,), c)
                p = strided(pre_ghost, (side,), c)
                for m in range(members):
                    half = 0.5 * there * jnp.exp(strided(lp_ghost, (side, m), c))
                    lam, frac = props(half, s)
                    half_perm[m, row, c] = half
                    L[0, m, row, c + 1] = lam
                    F[0, m, row, c + 1] = frac
                    Q[0, m, row, c + 1] = p

    def slab(field, k, m, r, c):
        return field[k, m, r, pl.ds(c, CHUNK + 2)]

    def face(k, m, r, mid):
        flux = (L[k, m, r, mid] + L[k, m, r + 1, mid]) * (Q[k, m, r, mid] - Q[k, m, r + 1, mid])
        return flux * jnp.where(flux > 0.0, F[k, m, r, mid], F[k, m, r + 1, mid])

    def saturate(k, m, r, lo, hi, new_below, new_above, keep):
        for c in range(lo, hi, CHUNK):
            mid = pl.ds(1 + c, CHUNK)
            lam_y, frac_y, press_y = slab(L, k, m, r, c), slab(F, k, m, r, c), slab(Q, k, m, r, c)
            lam, frac, press = lam_y[1:-1], frac_y[1:-1], press_y[1:-1]
            flux = (lam_y[:-1] + lam_y[1:]) * (press_y[:-1] - press_y[1:])
            along = flux * jnp.where(flux > 0.0, frac_y[:-1], frac_y[1:])
            outflow = along[1:] - along[:-1]
            here = pl.ds(c, CHUNK)
            below = face(k, m, r - 1, mid) if new_below else faces[m, r - 1, here]
            above = face(k, m, r, mid) if new_above else faces[m, r, here]
            if keep and new_below:
                faces[m, r - 1, here] = below
            if keep and new_above:
                faces[m, r, here] = above
            outflow = outflow + (above - below)
            lam_next = pltpu.roll(lam, nz - 1, 2)
            frac_next = pltpu.roll(frac, nz - 1, 2)
            press_next = pltpu.roll(press, nz - 1, 2)
            flux = (lam + lam_next) * inner * (press - press_next)
            along = flux * jnp.where(flux > 0.0, frac, frac_next)
            outflow = outflow + (along - pltpu.roll(along, 1, 2))
            outflow = outflow + ends * jnp.maximum(lam * press, 0.0) * frac
            source = src[r - 1, pl.ds(c, CHUNK)]
            water = jnp.maximum(source, 0.0) + jnp.minimum(source, 0.0) * frac
            s = jnp.clip(S[k, m, r, mid] + time_step * (water - outflow), 0.0, 1.0)
            lam, frac = props(half_perm[m, r, pl.ds(c, CHUNK)], s)
            S[k + 1, m, r, mid] = s
            L[k + 1, m, r, mid] = lam
            F[k + 1, m, r, mid] = frac

    def saturate_pads(k, m, r):
        pads(L, k + 1, m, r)
        pads(F, k + 1, m, r)

    def pressure(k, m, r, lo, hi):
        for c in range(lo, hi, CHUNK):
            mid = pl.ds(1 + c, CHUNK)
            lam_y, press_y = slab(L, k + 1, m, r, c), slab(Q, k, m, r, c)
            both_y = lam_y * press_y
            lam, press = lam_y[1:-1], press_y[1:-1]
            numer = press + src[r - 1, pl.ds(c, CHUNK)] + both_y[2:] + both_y[:-2]
            lam_sum = lam_y[2:] + lam_y[:-2]
            press_sum = press_y[2:] + press_y[:-2]
            others = [(L[k + 1, m, row, mid], Q[k, m, row, mid]) for row in (r - 1, r + 1)]
            others.append((pltpu.roll(lam, 1, 2) * not_first, pltpu.roll(press, 1, 2) * not_first))
            others.append((pltpu.roll(lam, nz - 1, 2) * inner, pltpu.roll(press, nz - 1, 2) * inner))
            for a, b in others:
                numer = numer + a * b
                lam_sum = lam_sum + a
                press_sum = press_sum + b
            Q[k + 1, m, r, mid] = (numer + lam * press_sum) * inverse_of(
                1.0 + 6.0 * lam + lam_sum
            )

    def pressure_pads(k, m, r):
        pads(Q, k + 1, m, r)

    def ghost_props(k, m, row, lo, hi):
        for c in range(lo, hi, CHUNK):
            mid = pl.ds(1 + c, CHUNK)
            lam, frac = props(half_perm[m, row, pl.ds(c, CHUNK)], S[k, m, row, mid])
            L[k, m, row, mid] = lam
            F[k, m, row, mid] = frac

    def s_halo(k, m, h):
        return lambda side: [halo(S, s_send, s_recv, k, m, h, side)]

    def p_halo(k, m, h):
        return lambda side: [halo(Q, p_send, p_recv, k, m, h, side)]

    def saturate_inside(k, m):
        saturate(k, m, 2, 0, yl, True, True, True)
        saturate_pads(k, m, 2)

        @pl.loop(3, width)
        def _(r):
            saturate(k, m, r, 0, yl, False, True, True)
            saturate_pads(k, m, r)

    def saturate_border(k, m, h):
        saturate(k, m, 1, h * piece, (h + 1) * piece, True, False, False)
        saturate(k, m, width, h * piece, (h + 1) * piece, False, True, False)
        if h == PARTS - 1:
            saturate_pads(k, m, 1)
            saturate_pads(k, m, width)

    def pressure_inside(k, m):
        @pl.loop(2, width)
        def _(r):
            pressure(k, m, r, 0, yl)
            pressure_pads(k, m, r)

    def pressure_border(k, m, h):
        @pl.loop(0, 2)
        def _(i):
            r = 1 + i * (width - 1)
            pressure(k, m, r, h * piece, (h + 1) * piece)
            if h == PARTS - 1:
                pressure_pads(k, m, r)

    def picked_rows(some):
        own = jnp.zeros((ens, LANES), jnp.float32)
        for r in some:
            found = jnp.zeros((ens, row_taps), jnp.float32)
            fields = Q[SWEEPS, :, r + 1, pl.ds(1, yl)].reshape(members * ny, nz)
            columns = split_dot(fields, z_hot[r])
            for m in range(members):
                picked = jnp.sum(columns[m * ny : (m + 1) * ny] * y_hot[r], axis=0, keepdims=True)
                found = jnp.where(iota((ens, row_taps), 0) == mem * members + m, picked, found)
            own = own + split_dot(found, tap_sum[r])
        return own

    for m in range(members):
        saturate_inside(0, m)
    first_ghosts()

    @pl.loop(0, SWEEPS)
    def _(k):
        for m in range(members):
            for h in range(PARTS):

                @pl.when(k > 0)
                def _(m=m, h=h):
                    each(p_halo(k, m, h), "wait_recv", False)

                saturate_border(k, m, h)
                each(s_halo(k + 1, m, h), "start", True)
            pressure_inside(k, m)

        @pl.when(k < width)
        def _():
            tables(k)

        @pl.when(k == SWEEPS - 1)
        def _():
            own_data()
            picks[...] = picked_rows(range(1, width - 1))

        for m in range(members):
            for h in range(PARTS):
                each(s_halo(k + 1, m, h), "wait_recv", False)

                @pl.loop(0, 2)
                def _(i, m=m, h=h):
                    ghost_props(k + 1, m, i * (width + 1), h * piece, (h + 1) * piece)

                pressure_border(k, m, h)

                @pl.when(k + 1 < SWEEPS)
                def _(m=m, h=h):
                    each(p_halo(k + 1, m, h), "start", True)

            @pl.when(k + 1 < SWEEPS)
            def _(m=m):
                saturate_inside(k + 1, m)

    pred[mem] = picks[...] + picked_rows((0, width - 1))

    def share(d):
        return remote(
            pred.at[mem], pred.at[mem], pred_send.at[d], pred_recv.at[d], (lax.rem(mem + d, n_mem), place)
        )

    for d in range(1, n_mem):
        share(d).start()
    value_own, var_own = obs_own[:SUB], obs_own[SUB : 2 * SUB]
    noise_own = obs_own[2 * SUB : 2 * SUB + ens]
    scale = jnp.where(iota((ens, LANES), 1) < local_obs, inflation * var_own, 1.0)
    inverse = jnp.where(iota((ens, LANES), 1) < local_obs, 1.0 / scale, 0.0)
    target_obs = value_own + jnp.sqrt(inflation * var_own) * noise_own
    for d in range(1, n_mem):
        share(d).wait_recv()
    predicted = pred[0]
    for a in range(1, n_mem):
        predicted = predicted + pred[a]
    dev = predicted - jnp.mean(predicted, axis=0, keepdims=True)
    resid = target_obs - predicted
    both = jnp.concatenate([dev, resid, jnp.zeros((LANES - 2 * ens, LANES), jnp.float32)], axis=0)
    gram[place] = lax.dot_general(
        dev * inverse, both, (((1,), (1,)), ((), ())), precision=HIGH, preferred_element_type=jnp.float32
    )

    def sum_part(d):
        return remote(
            gram.at[place],
            gram.at[place],
            gram_send.at[d],
            gram_recv.at[d],
            (mem, lax.rem(place + d, n_space)),
        )

    for d in range(1, n_space):
        sum_part(d).start()
    each(first, "wait_send", True)
    for d in range(1, n_mem):
        column(d).wait_send()
        share(d).wait_send()

    @pl.loop(1, SWEEPS + 1)
    def _(k):
        for m in range(members):
            for h in range(PARTS):
                each(s_halo(k, m, h), "wait_send", True)

                @pl.when(k < SWEEPS)
                def _(m=m, h=h):
                    each(p_halo(k, m, h), "wait_send", True)
    for d in range(1, n_mem):
        column(d).wait_recv()
    for d in range(1, n_space):
        sum_part(d).wait_recv()
    for d in range(1, n_space):
        sum_part(d).wait_send()
    whole = gram[0]
    for a in range(1, n_space):
        whole = whole + gram[a]

    row_id = iota((ens, LANES), 0)
    lane_id = iota((ens, LANES), 1)
    table = whole / (ens - 1) + as_float(row_id == lane_id)
    for i in range(ens):
        pivot_row = table[i : i + 1, :] / table[i : i + 1, i : i + 1]
        table = jnp.where(row_id == i, pivot_row, table - table[:, i : i + 1] * pivot_row)
    mixing = (
        table - jnp.mean(table, axis=0, keepdims=True) + as_float(row_id + ens == lane_id)
    )
    for m in range(ens):
        factors = [
            jnp.broadcast_to(mixing[j : j + 1, ens + m : ens + m + 1], (SUB, nz)) for j in range(ens)
        ]
        for r in range(width):
            for c in range(0, part, SUB):
                total = factors[0] * cols[0, r, pl.ds(c, SUB)]
                for j in range(1, ens):
                    total = total + factors[j] * cols[j, r, pl.ds(c, SUB)]
                out[m, r, pl.ds(c, SUB)] = total


def body(
    log_perm,
    saturation,
    pressure_init,
    wells,
    well_rate,
    obs_index,
    obs_weight,
    obs_value,
    obs_var,
    noise,
):
    n_mem = lax.axis_size("mem")
    n_space = lax.axis_size("space")
    members, width, ny, nz = log_perm.shape
    ens = members * n_mem
    yl = ny // SUB
    part = ny // n_mem
    row_taps = obs_index.size // (width * n_space)
    operands = (
        log_perm,
        saturation,
        pressure_init,
        wells[None],
        well_rate[None],
        obs_index.T,
        obs_weight.T,
        obs_value[None],
        obs_var[None],
        noise,
    )
    vmem = pl.BlockSpec(memory_space=pltpu.VMEM)
    state = pltpu.VMEM((SWEEPS + 1, members, width + 2, yl + 2, SUB, nz), jnp.float32)
    dma = pltpu.SemaphoreType.DMA
    return pl.pallas_call(
        functools.partial(kernel, n_mem, n_space),
        out_shape=jax.ShapeDtypeStruct((ens, width, part, nz), jnp.float32),
        in_specs=[pl.BlockSpec(memory_space=pltpu.HBM)] * 10,
        out_specs=vmem,
        scratch_shapes=[
            *[pltpu.VMEM(a.shape, a.dtype) for a in operands],
            pltpu.VMEM((width, nz, row_taps), jnp.float32),
            pltpu.VMEM((width, ny, row_taps), jnp.float32),
            pltpu.VMEM((width, row_taps, LANES), jnp.float32),
            pltpu.VMEM((2 * SUB + 16, LANES), jnp.float32),
            dma((11,)),
            state,
            state,
            state,
            state,
            pltpu.VMEM((members, width + 2, yl, SUB, nz), jnp.float32),
            pltpu.VMEM((width, yl, SUB, nz), jnp.float32),
            pltpu.VMEM((members, width, yl, SUB, nz), jnp.float32),
            pltpu.VMEM((ens, LANES), jnp.float32),
            pltpu.VMEM((2, members, ny, nz), jnp.float32),
            pltpu.VMEM((2, ny, nz), jnp.float32),
            pltpu.VMEM((2, ny, nz), jnp.float32),
            pltpu.VMEM((ens, width, part, nz), jnp.float32),
            pltpu.VMEM((n_mem, ens, LANES), jnp.float32),
            pltpu.VMEM((n_space, ens, LANES), jnp.float32),
            dma((2, 3)),
            dma((2, 3)),
            dma((SWEEPS + 1, members, PARTS, 2)),
            dma((SWEEPS + 1, members, PARTS, 2)),
            dma((SWEEPS + 1, members, PARTS, 2)),
            dma((SWEEPS + 1, members, PARTS, 2)),
            dma((n_mem,)),
            dma((n_mem,)),
            dma((n_mem,)),
            dma((n_mem,)),
            dma((n_space,)),
            dma((n_space,)),
        ],
        compiler_params=pltpu.CompilerParams(
            collective_id=0, has_side_effects=True, vmem_limit_bytes=62 * 1024 * 1024
        ),
    )(*operands)


def solution(mesh):
    placed = (
        P("mem", "space", None, None),
        P("space", None, None),
        P("space", None, None),
        P(),
        P(),
        P(),
        P(),
        P(),
        P(),
        P(),
    )
    return jax.shard_map(
        body, mesh=mesh, in_specs=placed, out_specs=P(None, "space", "mem", None), check_vma=False
    )
```
